512 devices in a mesh: dp: 16 (over z_lo, core), fsdp: 32 (over x, z_hi, y).
Axes of the slice: x: 4, y: 4, z: 16 (z_hi: 2, z_lo: 8; z = z_hi * 8 + z_lo), core: 2. Of those that a mesh axis runs over, the one named last changes fastest.
Arguments:
- hidden_input: bfloat16 [16, 2, 4096, 8192], P('dp', None, 'fsdp'), may hold values from -6 to 6
- readout: bfloat16 [16, 2, 4096, 512], P('dp', None, 'fsdp'), may hold values from -0.26367188 to 0.26367188
- response: int32 [16, 2, 4096], P('dp', None, 'fsdp'), may hold values from 0 to 1, as said below
- value_matrix: bfloat16 [8192, 512], P('fsdp'), may hold values from -0.0625 to 0.0625
- adapter_down: bfloat16 [8192, 64], P('fsdp'), may hold values from -0.0625 to 0.0625
- adapter_up: bfloat16 [64, 512], replicated, may hold values from -0.037353516 to 0.037353516
Outputs:
- down_gradient: float32 [8192, 64], P('fsdp')
- grad_b_t: float32 [512, 64], P('fsdp')
- losses: float32 [16], P('dp')
- margins: float32 [16], P('dp')
The draws below stay inside these ranges and needn't reach their ends.
Inputs may be any that keep to these rules, and one draw needn't show every extreme that they name: `response`: each sequence's 1s form one contiguous run of tokens that starts between 512 and 2048 and ends between 3072 and 4096.
All inputs are finite; a program needn't handle non-finite values.
Results may differ from the reference program's by a relative error of at most 0.0055.
Values may be sent and summed in bfloat16 or wider, within the bound.
No kernel may reach another device: no remote copies, remote signals or barrier semaphores. Data moves between devices by JAX's collectives and lax.ppermute only.
A program may use at most 64 MiB of HBM per device.

```python
import jax
import jax.numpy as jnp
from jax import lax

MODEL_WIDTH = 8192
VALUE_FEATURES = 512
ADAPTER_RANK = 64
LEN = 4096
PAIRS = 16


def draw_response(key, part):
    key = jax.random.fold_in(key, 7)
    first_key, second_key = jax.random.split(key)
    starts = jax.random.randint(first_key, (PAIRS, 2, 1), LEN // 8, LEN // 2 + 1)
    finish = jax.random.randint(second_key, (PAIRS, 2, 1), 3 * LEN // 4, LEN + 1)
    places = jnp.arange(LEN, dtype=jnp.int32)[None, None, :]
    inside = jnp.logical_and(places >= starts, places < finish)
    return inside.astype(jnp.int32)


def steps_of(own_key, dims, cuts, low, high):
    level = 1.0
    for axis_at, shards_of in cuts:
        steps = jax.random.uniform(jax.random.fold_in(jax.random.fold_in(own_key, 6), axis_at), (shards_of,), jnp.float32, low / len(cuts), high / len(cuts))
        level = level * jnp.repeat(jnp.exp(steps), dims[axis_at] // shards_of).reshape((-1,) + (1,) * (len(dims) - 1 - axis_at))
    return level


def bell_draw(stream_key, shape, deviation, reach, cuts=(), kind=jnp.bfloat16):
    gain = steps_of(stream_key, shape, cuts, -0.22, 0.18) if cuts else 1.0
    values = jax.random.normal(stream_key, shape, jnp.float32) * deviation * gain
    return jnp.minimum(jnp.maximum(values, -reach), reach).astype(kind)


def setup_inputs(seed: int = 0) -> dict:
    key_list = jax.random.split(jax.random.key(seed), 7)
    hidden_input = bell_draw(key_list[0], (PAIRS, 2, LEN, MODEL_WIDTH), 1.0, 6.0, ((0, 16), (2, 32)))
    readout = bell_draw(key_list[1], (PAIRS, 2, LEN, VALUE_FEATURES), (1.0 / VALUE_FEATURES ** 0.5), 0.26367188, ((0, 16), (2, 32)))
    response = draw_response(jax.random.fold_in(key_list[6], 71), 0)
    value_matrix = bell_draw(key_list[3], (MODEL_WIDTH, VALUE_FEATURES), MODEL_WIDTH ** -0.5, 0.0625, ((0, 32),))
    adapter_down = bell_draw(key_list[4], (MODEL_WIDTH, ADAPTER_RANK), MODEL_WIDTH ** -0.5, 0.0625, ((0, 32),))
    adapter_up = bell_draw(key_list[5], (ADAPTER_RANK, VALUE_FEATURES), (0.05 / ADAPTER_RANK ** 0.5), 0.037353516)
    return {"hidden_input": hidden_input, "readout": readout, "response": response, "value_matrix": value_matrix, "adapter_down": adapter_down, "adapter_up": adapter_up}


DPO_BETA = 0.5
ADAPTER_SCALE = 2.0


def pairwise_terms(token_pair, pair_readout, pair_mask, value_matrix, adapter_down, adapter_up):
    seq_total = token_pair.shape[1]
    token_row_block = token_pair.reshape(2 * seq_total, token_pair.shape[2])
    base_output = jnp.dot(token_row_block, value_matrix, preferred_element_type=jnp.float32)
    lowrank_output = jnp.dot(token_row_block, adapter_down, preferred_element_type=jnp.float32).astype(jnp.bfloat16)
    policy_score = base_output + ADAPTER_SCALE * jnp.dot(lowrank_output, adapter_up, preferred_element_type=jnp.float32)
    read_f = pair_readout.reshape(2 * seq_total, -1).astype(jnp.float32)
    mask_f = pair_mask.reshape(2 * seq_total).astype(jnp.float32)
    t_pol = jnp.tanh(policy_score)
    t_ref = jnp.tanh(base_output)
    scores = jnp.sum(read_f * (t_pol - t_ref), axis=1) * mask_f
    ratio = jnp.sum(scores.reshape(2, seq_total), axis=1)
    reward_margin = DPO_BETA * (ratio[0] - ratio[1])
    pair_loss_total = jax.nn.softplus(-reward_margin)
    gate = jax.nn.sigmoid(-reward_margin)
    coef = DPO_BETA * gate * jnp.array([-1.0, 1.0], jnp.float32)
    coef_rows = jnp.repeat(coef, seq_total)
    hidden_gradient = (coef_rows[:, None] * mask_f[:, None] * read_f * (1.0 - t_pol * t_pol)).astype(jnp.bfloat16)
    up_gradient_flipped = ADAPTER_SCALE * lax.dot_general(hidden_gradient, lowrank_output, (((0,), (0,)), ((), ())), preferred_element_type=jnp.float32)
    lowrank_gradient = (ADAPTER_SCALE * lax.dot_general(hidden_gradient, adapter_up, (((1,), (1,)), ((), ())), preferred_element_type=jnp.float32)).astype(jnp.bfloat16)
    down_gradient = lax.dot_general(token_row_block, lowrank_gradient, (((0,), (0,)), ((), ())), preferred_element_type=jnp.float32)
    return down_gradient, up_gradient_flipped, pair_loss_total, reward_margin


def reference(hidden_input, readout, response, value_matrix, adapter_down, adapter_up):
    def step(totals, items):
        token_pair, pair_readout, pair_mask = items
        down_gradient, up_gradient_flipped, pair_loss_total, reward_margin = pairwise_terms(token_pair, pair_readout, pair_mask, value_matrix, adapter_down, adapter_up)
        return (totals[0] + down_gradient, totals[1] + up_gradient_flipped), (pair_loss_total, reward_margin)

    start_sums = (jnp.zeros((MODEL_WIDTH, ADAPTER_RANK), jnp.float32), jnp.zeros((VALUE_FEATURES, ADAPTER_RANK), jnp.float32))
    sums, outs = lax.scan(step, start_sums, (hidden_input, readout, response))
    return sums[0], sums[1], outs[0], outs[1]
```

```python
import jax
import jax.numpy as jnp
import numpy as np
from jax import lax
from jax.experimental import pallas as pl
from jax.experimental.pallas import tpu as pltpu
from jax.sharding import Mesh, PartitionSpec as P

DPO_BETA = 0.5
ADAPTER_SCALE = 2.0
BF16 = jnp.bfloat16
F32 = jnp.float32
LANES = 128
X, Y, ZH, ZL = 4, 4, 2, 8
XY = ("x", "y")
ZZ = ("zl", "zh")
EXTRA = 16


def vmem():
    return pl.BlockSpec(memory_space=pltpu.VMEM)


def params():
    return pltpu.CompilerParams(vmem_limit_bytes=50 * 1024 * 1024)


def pieces(total, shape):
    full = jnp.broadcast_to(total, shape)
    high = full.astype(BF16).astype(F32)
    rest = full - high
    middle = rest.astype(BF16).astype(F32)
    low = rest - middle
    lane = lax.broadcasted_iota(jnp.int32, shape, 1)
    zero = jnp.zeros(shape, F32)
    return jnp.where(lane == 0, high, jnp.where(lane == 1, middle, jnp.where(lane == 2, low, zero)))


def order_kernel(where_ref, hidden_ref, out_ref):
    core, zh = where_ref[0], where_ref[1]
    at = 0
    for core_rel in range(2):
        for zh_rel in range(ZH):
            for x in range(X):
                for y in range(Y):
                    own_core = jnp.where(core_rel == 0, core, 1 - core)
                    own_zh = jnp.where(zh_rel == 0, zh, 1 - zh)
                    start = (((x * ZH + own_zh) * Y + y) * 2 + own_core) * LANES
                    out_ref[core_rel, :, at * LANES : (at + 1) * LANES] = hidden_ref[
                        :, pl.ds(pl.multiple_of(start, LANES), LANES)
                    ]
                    at = (at + 1) % (ZH * X * Y)


def forward_kernel(first, *refs):
    if first:
        mine_ref, other_ref, weight_ref, out_ref = refs
    else:
        mine_ref, other_ref, weight_ref, before_ref, out_ref = refs
    step = pl.program_id(0)
    tokens = mine_ref.shape[0]
    features = weight_ref.shape[2]
    sources = weight_ref.shape[0]
    value = weight_ref[:, :LANES, :].reshape(sources * LANES, features)
    down_t = jnp.concatenate(
        [
            jnp.concatenate(
                [weight_ref[s, LANES:, g * LANES : (g + 1) * LANES] for g in range(features // LANES)], axis=0
            )
            for s in range(sources)
        ],
        axis=1,
    )
    down_t = jnp.concatenate([down_t, jnp.zeros_like(down_t)], axis=0)
    for at, ref in enumerate((mine_ref, other_ref)):
        rows = slice(at * tokens, (at + 1) * tokens)
        base = jnp.dot(ref[...], value, preferred_element_type=F32)
        low = lax.dot_general(ref[...], down_t, (((1,), (1,)), ((), ())), preferred_element_type=F32)

        @pl.when(step == 0)
        def _():
            if first:
                out_ref[rows, :features] = base
                out_ref[rows, features:] = low
            else:
                out_ref[rows, :features] = before_ref[rows, :features] + base
                out_ref[rows, features:] = before_ref[rows, features:] + low

        @pl.when(step != 0)
        def _():
            out_ref[rows, :features] += base
            out_ref[rows, features:] += low


def forward(mine, other, weights, part, before=None):
    tokens = mine.shape[0]
    features = weights.shape[2]
    steps = 4
    sources = X * Y // steps
    wide = sources * LANES
    specs = [
        pl.BlockSpec((tokens, wide), lambda i: (0, part * steps + i)),
        pl.BlockSpec((tokens, wide), lambda i: (0, part * steps + i)),
        pl.BlockSpec((sources,) + weights.shape[1:], lambda i: (i, 0, 0)),
    ]
    given = [mine, other, weights]
    whole = pl.BlockSpec((2 * tokens, features + LANES), lambda i: (0, 0))
    if before is not None:
        specs.append(whole)
        given.append(before)
    return pl.pallas_call(
        lambda *refs: forward_kernel(before is None, *refs),
        grid=(steps,),
        in_specs=specs,
        out_specs=whole,
        out_shape=jax.ShapeDtypeStruct((2 * tokens, features + LANES), F32),
        compiler_params=params(),
        name="forward",
    )(*given)


def middle_kernel(mine_ref, other_ref, hidden_ref, read_ref, mask_ref, up_ref, out_ref):
    tokens, features = read_ref.shape
    rank = up_ref.shape[0] // 2
    base = mine_ref[:tokens, :features] + other_ref[:, :features]
    low = mine_ref[:tokens, features:] + other_ref[:, features:]
    low_b = low.astype(BF16)
    policy = base + ADAPTER_SCALE * jnp.dot(low_b, up_ref[...], preferred_element_type=F32)
    read = read_ref[...].astype(F32)
    sign = jnp.where(lax.broadcasted_iota(jnp.int32, (tokens, 1), 0) < tokens // 2, 1.0, -1.0)
    signed = mask_ref[...] * sign
    t_pol = jnp.tanh(policy)
    t_ref = jnp.tanh(base)
    scores = jnp.sum(read * (t_pol - t_ref), axis=1, keepdims=True) * signed
    total = jnp.sum(scores, axis=0, keepdims=True)
    grad = ((-DPO_BETA * signed) * read * (1.0 - t_pol * t_pol)).astype(BF16)
    low_grad_t = (
        ADAPTER_SCALE
        * lax.dot_general(up_ref[:rank, :], grad, (((1,), (1,)), ((), ())), preferred_element_type=F32)
    ).astype(BF16)
    twice = (low + pltpu.roll(low, rank, 1)).astype(BF16)
    up_grad = ADAPTER_SCALE * lax.dot_general(
        grad, twice, (((0,), (0,)), ((), ())), preferred_element_type=F32
    )
    wide = 2 * LANES
    part = features // (X * ZH * Y)
    lane = lax.broadcasted_iota(jnp.int32, (EXTRA, LANES), 1)
    sent = pieces(total, (EXTRA, LANES)).astype(BF16)
    for x in range(X):
        for y in range(Y):
            to = x * Y + y
            places = [(x * ZH + zh) * Y + y for zh in range(ZH)]
            for zh, s in enumerate(places):
                out_ref[to, zh * rank : (zh + 1) * rank, :] = jnp.dot(
                    low_grad_t, hidden_ref[:, s * wide : (s + 1) * wide], preferred_element_type=F32
                ).astype(BF16)
            both = jnp.where(
                lane < rank,
                up_grad[places[0] * part : (places[0] + 1) * part, :],
                up_grad[places[1] * part : (places[1] + 1) * part, :],
            )
            out_ref[to, ZH * rank :, :LANES] = both.astype(BF16)
            out_ref[to, ZH * rank :, LANES:] = sent


def plane_kernel(got_ref, out_ref):
    rank = (got_ref.shape[1] - EXTRA) // ZH
    rows = rank // ZL
    total = got_ref[0].astype(F32)
    for s in range(1, got_ref.shape[0]):
        total = total + got_ref[s].astype(F32)
    first = ZH * rank
    margin = jnp.sum(total[first : first + 1, LANES:], axis=1, keepdims=True)
    sent = pieces(margin, (8, LANES))
    lane = lax.broadcasted_iota(jnp.int32, (8, LANES), 1)
    upper = total[first : first + 8, :LANES]
    lower = total[first + 8 : first + 16, :LANES]
    packed = [
        jnp.where(lane < rank, upper, pltpu.roll(lower, rank, 1)),
        jnp.where(lane < rank, pltpu.roll(upper, rank, 1), lower),
    ]
    for zl in range(ZL):
        for zh in range(ZH):
            start = zh * rank + zl * rows
            tail = jnp.concatenate([packed[zh], sent], axis=1)
            out_ref[zl * ZH + zh] = jnp.concatenate(
                [total[start : start + rows, :], tail], axis=0
            ).astype(BF16)


def gate_kernel(got_ref, out_ref, diff_ref):
    total = None
    for zl in range(ZL):
        pair = got_ref[zl * ZH].astype(F32) + got_ref[zl * ZH + 1].astype(F32)
        diff = jnp.sum(pair[8:9, LANES:], axis=1, keepdims=True)
        gate = 1.0 / (1.0 + jnp.exp(DPO_BETA * diff))
        total = gate * pair if total is None else total + gate * pair
        diff_ref[zl : zl + 1, :] = jnp.broadcast_to(diff, (1, LANES))
    out_ref[...] = total


def shards(hidden_input, readout, response, value_matrix, adapter_down, adapter_up):
    seq_rows, width = hidden_input.shape[2:]
    tokens = 2 * seq_rows
    features = value_matrix.shape[1]
    rank = adapter_down.shape[1]
    core, zh, zl = lax.axis_index("core"), lax.axis_index("zh"), lax.axis_index("zl")
    hidden = hidden_input.reshape(tokens, width)

    value_half = lax.dynamic_slice_in_dim(value_matrix, core * LANES, LANES, 0)
    down_half = lax.dynamic_slice_in_dim(adapter_down, core * LANES, LANES, 0)
    packed = down_half.T.reshape(features // LANES, EXTRA, LANES).transpose(1, 0, 2).reshape(EXTRA, features)
    weights = jnp.concatenate([value_half, packed], axis=0)
    spots = [(a, c, b, e, d) for a in range(ZL) for c in range(2) for b in range(X) for e in range(ZH) for d in range(Y)]
    sizes = (ZL, 2, X, ZH, Y)
    axes = ("zl", "core", "x", "zh", "y")
    flat = lambda p: int(np.ravel_multi_index(p, sizes))
    swap_zh = [(flat(p), flat((p[0], p[1], p[2], 1 - p[3], p[4]))) for p in spots]
    swap_core = [(0, 1), (1, 0)]

    weights_far = lax.ppermute(weights, axes, swap_zh)
    spread = lambda w: lax.all_to_all(jnp.broadcast_to(w[None], (X * Y,) + w.shape), XY, 0, 0)
    near = spread(weights)

    halves = pl.pallas_call(
        order_kernel,
        in_specs=[pl.BlockSpec(memory_space=pltpu.SMEM), vmem()],
        out_specs=vmem(),
        out_shape=jax.ShapeDtypeStruct((2, tokens, width // 2), BF16),
        compiler_params=params(),
        name="order",
    )(jnp.stack([core, zh]).astype(jnp.int32), hidden)
    mine = halves[0]
    other = lax.ppermute(halves[1], "core", swap_core)

    far = spread(weights_far)
    part = forward(mine, other, near, 0)
    part = forward(mine, other, far, 1, part)
    from_other = lax.ppermute(part[tokens:], "core", swap_core)

    read = readout.reshape(tokens, features)
    mask = response.reshape(tokens, 1).astype(F32)
    up = jnp.pad(adapter_up, ((0, rank), (0, 0)))
    wide = width // (X * ZH * Y)
    sends = pl.pallas_call(
        middle_kernel,
        in_specs=[vmem()] * 6,
        out_specs=vmem(),
        out_shape=jax.ShapeDtypeStruct((X * Y, ZH * rank + EXTRA, wide), BF16),
        compiler_params=params(),
        name="middle",
    )(part, from_other, hidden, read, mask, up)
    got = lax.all_to_all(sends, XY, 0, 0)
    along = pl.pallas_call(
        plane_kernel,
        in_specs=[vmem()],
        out_specs=vmem(),
        out_shape=jax.ShapeDtypeStruct((ZL * ZH, 16, wide), BF16),
        compiler_params=params(),
        name="plane",
    )(got)
    got = lax.all_to_all(along, ZZ, 0, 0)
    gated, diffs = pl.pallas_call(
        gate_kernel,
        in_specs=[vmem()],
        out_specs=[vmem(), vmem()],
        out_shape=[jax.ShapeDtypeStruct((16, wide), F32), jax.ShapeDtypeStruct((ZL, LANES), F32)],
        compiler_params=params(),
        name="gate",
    )(got)
    summed = lax.psum(gated, "core")
    rows = rank // ZL
    all_rows = lax.all_to_all(jnp.broadcast_to(summed[None, :rows], (ZL, rows, wide)), "zl", 0, 0)
    down_gradient = all_rows.reshape(rank, wide).T
    up_part = jnp.concatenate([summed[8:16, :rank], summed[8:16, rank : 2 * rank]], axis=0)
    margin = DPO_BETA * lax.dynamic_slice(diffs, (zl, 0), (1, 1)).reshape(1)
    return down_gradient, up_part, jax.nn.softplus(-margin), margin


def solution(mesh):
    fine = Mesh(np.asarray(mesh.devices).reshape(ZL, 2, X, ZH, Y), ("zl", "core", "x", "zh", "y"))
    dp, fsdp = ("zl", "core"), ("x", "zh", "y")
    placed = (
        P(dp, None, fsdp, None),
        P(dp, None, fsdp, None),
        P(dp, None, fsdp),
        P(fsdp, None),
        P(fsdp, None),
        P(),
    )
    return jax.shard_map(
        shards,
        mesh=fine,
        in_specs=placed,
        out_specs=(P(fsdp, None), P(fsdp, None), P(dp), P(dp)),
        check_vma=False,
    )
```

```python
import jax
import jax.numpy as jnp
import numpy as np
from jax import lax
from jax.experimental import pallas as pl
from jax.experimental.pallas import tpu as pltpu
from jax.sharding import Mesh, PartitionSpec as P

DPO_BETA = 0.5
ADAPTER_SCALE = 2.0
BF16 = jnp.bfloat16
F32 = jnp.float32
LANES = 128
X, Y, ZH, ZL = 4, 4, 2, 8
XY = ("x", "y")
ZZ = ("zl", "zh")
EXTRA = 16


def vmem():
    return pl.BlockSpec(memory_space=pltpu.VMEM)


def params():
    return pltpu.CompilerParams(vmem_limit_bytes=28 * 1024 * 1024)


def pieces(total, shape):
    full = jnp.broadcast_to(total, shape)
    high = full.astype(BF16).astype(F32)
    rest = full - high
    middle = rest.astype(BF16).astype(F32)
    low = rest - middle
    lane = lax.broadcasted_iota(jnp.int32, shape, 1)
    zero = jnp.zeros(shape, F32)
    return jnp.where(lane == 0, high, jnp.where(lane == 1, middle, jnp.where(lane == 2, low, zero)))


def order_kernel(where_ref, hidden_ref, mine_ref, other_ref):
    core, zh = where_ref[0], where_ref[1]
    for own_core, out_ref in ((core, mine_ref), (1 - core, other_ref)):
        at = 0
        for own_zh in (zh, 1 - zh):
            for x, y in BLOCKS:
                start = (((x * ZH + own_zh) * Y + y) * 2 + own_core) * LANES
                out_ref[:, at * LANES : (at + 1) * LANES] = hidden_ref[
                    :, pl.ds(pl.multiple_of(start, LANES), LANES)
                ]
                at += 1


def unpacked(weight_ref):
    sources, _, features = weight_ref.shape
    value = weight_ref[:, :LANES, :].reshape(sources * LANES, features)
    down_t = [
        jnp.concatenate(
            [weight_ref[s, LANES:, g * LANES : (g + 1) * LANES] for g in range(features // LANES)], axis=0
        )
        for s in range(sources)
    ]
    return value, down_t


def low_part(hidden, down_t):
    down_t = jnp.concatenate(down_t, axis=1)
    down_t = jnp.concatenate([down_t, jnp.zeros((LANES - down_t.shape[0], down_t.shape[1]), BF16)], axis=0)
    return lax.dot_general(hidden, down_t, (((1,), (1,)), ((), ())), preferred_element_type=F32)


def near_kernel(mine_ref, other_ref, weight_ref, out_mine_ref, out_other_ref):
    features = weight_ref.shape[2]
    value, down_t = unpacked(weight_ref)
    for ref, out_ref in ((mine_ref, out_mine_ref), (other_ref, out_other_ref)):
        hidden = ref[...]
        out_ref[:, :features] = jnp.dot(hidden, value, preferred_element_type=F32)
        out_ref[:, features:] = low_part(hidden, down_t)


def far_kernel(hidden_ref, first_ref, second_ref, before_ref, out_ref):
    half = first_ref.shape[2]
    first, first_t = unpacked(first_ref)
    second, second_t = unpacked(second_ref)
    hidden = hidden_ref[...]
    turned = jnp.concatenate(
        [hidden[:, BLOCKS.index(p) * LANES : (BLOCKS.index(p) + 1) * LANES] for p in TURNED], axis=1
    )
    down_t = [jnp.concatenate([first_t[k], second_t[TURNED.index(p)]], axis=0) for k, p in enumerate(BLOCKS)]
    out_ref[:, :half] = before_ref[:, :half] + jnp.dot(hidden, first, preferred_element_type=F32)
    out_ref[:, half : 2 * half] = before_ref[:, half : 2 * half] + jnp.dot(
        turned, second, preferred_element_type=F32
    )
    out_ref[:, 2 * half :] = before_ref[:, 2 * half :] + low_part(hidden, down_t)


def half_of(tokens, half, part):
    return pl.BlockSpec((tokens, half), lambda i: (0, part))


def whole(shape):
    return pl.BlockSpec(shape, lambda i: (0,) * len(shape))


def near_forward(mine, other, weights):
    tokens, half = mine.shape[0], mine.shape[1] // 2
    out = (tokens, weights.shape[2] + LANES)
    return pl.pallas_call(
        near_kernel,
        grid=(1,),
        in_specs=[half_of(tokens, half, 0), half_of(tokens, half, 0), whole(weights.shape)],
        out_specs=[whole(out)] * 2,
        out_shape=[jax.ShapeDtypeStruct(out, F32)] * 2,
        compiler_params=params(),
        name="near",
    )(mine, other, weights)


def far_forward(hidden, first, second, before):
    tokens, half = hidden.shape[0], hidden.shape[1] // 2
    return pl.pallas_call(
        far_kernel,
        grid=(1,),
        in_specs=[half_of(tokens, half, 1), whole(first.shape), whole(second.shape), whole(before.shape)],
        out_specs=whole(before.shape),
        out_shape=jax.ShapeDtypeStruct(before.shape, F32),
        compiler_params=params(),
        name="far",
    )(hidden, first, second, before)


EVEN_FIRST = ((0, 1), (2, 3)), ((1, 2), (0, 3))
ODD_FIRST = ((1, 2), (3, 0)), ((1, 0), (2, 3))


def block_order(first):
    return [(a[i], b[j]) for a in first for b in first for i in range(2) for j in range(2)]


BLOCKS = block_order(EVEN_FIRST[0])
TURNED = block_order(ODD_FIRST[0])


def two_step_gather(w, tilings):
    for pairs in tilings:
        groups = [[a * Y + b for a in first for b in second] for first in pairs for second in pairs]
        w = lax.all_to_all(jnp.broadcast_to(w[None], (4,) + w.shape), XY, 0, 0, axis_index_groups=groups)
    return w.reshape((X * Y,) + w.shape[2:])


def middle_kernel(mine_ref, other_ref, hidden_ref, read_ref, mask_ref, up_ref, out_ref):
    tokens, features = read_ref.shape
    rank = up_ref.shape[0] // 2
    base = mine_ref[:, :features] + other_ref[:, :features]
    low = mine_ref[:, features:] + other_ref[:, features:]
    low_b = low.astype(BF16)
    policy = base + ADAPTER_SCALE * jnp.dot(low_b, up_ref[...], preferred_element_type=F32)
    read = read_ref[...].astype(F32)
    sign = jnp.where(lax.broadcasted_iota(jnp.int32, (tokens, 1), 0) < tokens // 2, 1.0, -1.0)
    signed = mask_ref[...] * sign
    t_pol = jnp.tanh(policy)
    t_ref = jnp.tanh(base)
    scores = jnp.sum(read * (t_pol - t_ref), axis=1, keepdims=True) * signed
    total = jnp.sum(scores, axis=0, keepdims=True)
    grad = ((-DPO_BETA * signed) * read * (1.0 - t_pol * t_pol)).astype(BF16)
    low_grad_t = (
        ADAPTER_SCALE
        * lax.dot_general(up_ref[:rank, :], grad, (((1,), (1,)), ((), ())), preferred_element_type=F32)
    ).astype(BF16)
    twice = (low + pltpu.roll(low, rank, 1)).astype(BF16)
    up_grad = ADAPTER_SCALE * lax.dot_general(
        grad, twice, (((0,), (0,)), ((), ())), preferred_element_type=F32
    )
    wide = 2 * LANES
    part = features // (X * ZH * Y)
    lane = lax.broadcasted_iota(jnp.int32, (EXTRA, LANES), 1)
    sent = pieces(total, (EXTRA, LANES)).astype(BF16)
    for x in range(X):
        for y in range(Y):
            to = x * Y + y
            places = [(x * ZH + zh) * Y + y for zh in range(ZH)]
            for zh, s in enumerate(places):
                out_ref[to, zh * rank : (zh + 1) * rank, :] = jnp.dot(
                    low_grad_t, hidden_ref[:, s * wide : (s + 1) * wide], preferred_element_type=F32
                ).astype(BF16)
            both = jnp.where(
                lane < rank,
                up_grad[places[0] * part : (places[0] + 1) * part, :],
                up_grad[places[1] * part : (places[1] + 1) * part, :],
            )
            out_ref[to, ZH * rank :, :LANES] = both.astype(BF16)
            out_ref[to, ZH * rank :, LANES:] = sent


def plane_kernel(got_ref, out_ref):
    rank = (got_ref.shape[1] - EXTRA) // ZH
    rows = rank // ZL
    total = got_ref[0].astype(F32)
    for s in range(1, got_ref.shape[0]):
        total = total + got_ref[s].astype(F32)
    first = ZH * rank
    margin = jnp.sum(total[first : first + 1, LANES:], axis=1, keepdims=True)
    sent = pieces(margin, (8, LANES))
    lane = lax.broadcasted_iota(jnp.int32, (8, LANES), 1)
    upper = total[first : first + 8, :LANES]
    lower = total[first + 8 : first + 16, :LANES]
    packed = [
        jnp.where(lane < rank, upper, pltpu.roll(lower, rank, 1)),
        jnp.where(lane < rank, pltpu.roll(upper, rank, 1), lower),
    ]
    for zl in range(ZL):
        for zh in range(ZH):
            start = zh * rank + zl * rows
            tail = jnp.concatenate([packed[zh], sent], axis=1)
            out_ref[zl * ZH + zh] = jnp.concatenate(
                [total[start : start + rows, :], tail], axis=0
            ).astype(BF16)


def gate_kernel(got_ref, out_ref, diff_ref):
    total = None
    for zl in range(ZL):
        pair = got_ref[zl * ZH].astype(F32) + got_ref[zl * ZH + 1].astype(F32)
        diff = jnp.sum(pair[8:9, LANES:], axis=1, keepdims=True)
        gate = 1.0 / (1.0 + jnp.exp(DPO_BETA * diff))
        total = gate * pair if total is None else total + gate * pair
        diff_ref[zl : zl + 1, :] = jnp.broadcast_to(diff, (1, LANES))
    out_ref[...] = total


def shards(hidden_input, readout, response, value_matrix, adapter_down, adapter_up):
    seq_rows, width = hidden_input.shape[2:]
    tokens = 2 * seq_rows
    features = value_matrix.shape[1]
    rank = adapter_down.shape[1]
    core, zh, zl = lax.axis_index("core"), lax.axis_index("zh"), lax.axis_index("zl")
    hidden = hidden_input.reshape(tokens, width)

    value_half = lax.dynamic_slice_in_dim(value_matrix, core * LANES, LANES, 0)
    down_half = lax.dynamic_slice_in_dim(adapter_down, core * LANES, LANES, 0)
    packed = down_half.T.reshape(features // LANES, EXTRA, LANES).transpose(1, 0, 2).reshape(EXTRA, features)
    weights = jnp.concatenate([value_half, packed], axis=0)
    spots = [(a, c, b, e, d) for a in range(ZL) for c in range(2) for b in range(X) for e in range(ZH) for d in range(Y)]
    sizes = (ZL, 2, X, ZH, Y)
    axes = ("zl", "core", "x", "zh", "y")
    flat = lambda p: int(np.ravel_multi_index(p, sizes))
    swap_zh = [(flat(p), flat((p[0], p[1], p[2], 1 - p[3], p[4]))) for p in spots]
    swap_core = [(0, 1), (1, 0)]

    weights_far = lax.ppermute(weights, axes, swap_zh)
    near = two_step_gather(weights, EVEN_FIRST)
    mine, for_other = pl.pallas_call(
        order_kernel,
        in_specs=[pl.BlockSpec(memory_space=pltpu.SMEM), vmem()],
        out_specs=[vmem(), vmem()],
        out_shape=[jax.ShapeDtypeStruct((tokens, width // 2), BF16)] * 2,
        compiler_params=params(),
        name="order",
    )(jnp.stack([core, zh]).astype(jnp.int32), hidden)
    other = lax.ppermute(for_other, "core", swap_core)
    near_mine, near_other = near_forward(mine, other, near)

    first = two_step_gather(weights_far[:, : features // 2], EVEN_FIRST)
    second = two_step_gather(weights_far[:, features // 2 :], ODD_FIRST)
    part_other = far_forward(other, first, second, near_other)
    from_other = lax.ppermute(part_other, "core", swap_core)
    part_mine = far_forward(mine, first, second, near_mine)

    read = readout.reshape(tokens, features)
    mask = response.reshape(tokens, 1).astype(F32)
    up = jnp.pad(adapter_up, ((0, rank), (0, 0)))
    wide = width // (X * ZH * Y)
    sends = pl.pallas_call(
        middle_kernel,
        in_specs=[vmem()] * 6,
        out_specs=vmem(),
        out_shape=jax.ShapeDtypeStruct((X * Y, ZH * rank + EXTRA, wide), BF16),
        compiler_params=params(),
        name="middle",
    )(part_mine, from_other, hidden, read, mask, up)
    got = lax.all_to_all(sends, XY, 0, 0)
    along = pl.pallas_call(
        plane_kernel,
        in_specs=[vmem()],
        out_specs=vmem(),
        out_shape=jax.ShapeDtypeStruct((ZL * ZH, 16, wide), BF16),
        compiler_params=params(),
        name="plane",
    )(got)
    got = lax.all_to_all(along, ZZ, 0, 0)
    gated, diffs = pl.pallas_call(
        gate_kernel,
        in_specs=[vmem()],
        out_specs=[vmem(), vmem()],
        out_shape=[jax.ShapeDtypeStruct((16, wide), F32), jax.ShapeDtypeStruct((ZL, LANES), F32)],
        compiler_params=params(),
        name="gate",
    )(got)
    summed = lax.psum(gated, "core")
    rows = rank // ZL
    all_rows = lax.all_to_all(jnp.broadcast_to(summed[None, :rows], (ZL, rows, wide)), "zl", 0, 0)
    down_gradient = all_rows.reshape(rank, wide).T
    up_part = jnp.concatenate([summed[8:16, :rank], summed[8:16, rank : 2 * rank]], axis=0)
    margin = DPO_BETA * lax.dynamic_slice(diffs, (zl, 0), (1, 1)).reshape(1)
    return down_gradient, up_part, jax.nn.softplus(-margin), margin


def solution(mesh):
    fine = Mesh(np.asarray(mesh.devices).reshape(ZL, 2, X, ZH, Y), ("zl", "core", "x", "zh", "y"))
    dp, fsdp = ("zl", "core"), ("x", "zh", "y")
    placed = (
        P(dp, None, fsdp, None),
        P(dp, None, fsdp, None),
        P(dp, None, fsdp),
        P(fsdp, None),
        P(fsdp, None),
        P(),
    )
    return jax.shard_map(
        shards,
        mesh=fine,
        in_specs=placed,
        out_specs=(P(fsdp, None), P(fsdp, None), P(dp), P(dp)),
        check_vma=False,
    )
```

```python
import jax
import jax.numpy as jnp
import numpy as np
from jax import lax
from jax.experimental import pallas as pl
from jax.experimental.pallas import tpu as pltpu
from jax.sharding import Mesh, PartitionSpec as P

DPO_BETA = 0.5
ADAPTER_SCALE = 2.0
BF16 = jnp.bfloat16
F32 = jnp.float32
LANES = 128
X, Y, ZH, ZL = 4, 4, 2, 8
XY = ("x", "y")
ZZ = ("zl", "zh")
EXTRA = 16


def vmem():
    return pl.BlockSpec(memory_space=pltpu.VMEM)


def params():
    return pltpu.CompilerParams(vmem_limit_bytes=28 * 1024 * 1024)


def pieces(total, shape):
    full = jnp.broadcast_to(total, shape)
    high = full.astype(BF16).astype(F32)
    rest = full - high
    middle = rest.astype(BF16).astype(F32)
    low = rest - middle
    lane = lax.broadcasted_iota(jnp.int32, shape, 1)
    zero = jnp.zeros(shape, F32)
    return jnp.where(lane == 0, high, jnp.where(lane == 1, middle, jnp.where(lane == 2, low, zero)))


def order_kernel(where_ref, hidden_ref, mine_ref, other_ref):
    core, zh = where_ref[0], where_ref[1]
    for own_core, out_ref in ((core, mine_ref), (1 - core, other_ref)):
        at = 0
        for own_zh in (zh, 1 - zh):
            for x in range(X):
                for y in range(Y):
                    start = (((x * ZH + own_zh) * Y + y) * 2 + own_core) * LANES
                    out_ref[:, at * LANES : (at + 1) * LANES] = hidden_ref[
                        :, pl.ds(pl.multiple_of(start, LANES), LANES)
                    ]
                    at += 1


def unpacked(weight_ref):
    sources, _, features = weight_ref.shape
    value = weight_ref[:, :LANES, :].reshape(sources * LANES, features)
    down_t = [
        jnp.concatenate([weight_ref[s, LANES:, g * LANES : (g + 1) * LANES] for s in range(sources)], axis=1)
        for g in range(features // LANES)
    ]
    return value, jnp.concatenate(down_t, axis=0)


def low_part(hidden, down_t):
    down_t = jnp.concatenate([down_t, jnp.zeros((LANES - down_t.shape[0], down_t.shape[1]), BF16)], axis=0)
    return lax.dot_general(hidden, down_t, (((1,), (1,)), ((), ())), preferred_element_type=F32)


def near_kernel(mine_ref, other_ref, first_ref, second_ref, out_mine_ref, out_other_ref):
    half = first_ref.shape[2]
    first, first_t = unpacked(first_ref)
    second, second_t = unpacked(second_ref)
    down_t = jnp.concatenate([first_t, second_t], axis=0)
    for ref, out_ref in ((mine_ref, out_mine_ref), (other_ref, out_other_ref)):
        hidden = ref[:, : first.shape[0]]
        out_ref[:, :half] = jnp.dot(hidden, first, preferred_element_type=F32)
        out_ref[:, half : 2 * half] = jnp.dot(hidden, second, preferred_element_type=F32)
        out_ref[:, 2 * half :] = low_part(hidden, down_t)


def far_kernel(hidden_ref, weight_ref, before_ref, out_ref):
    features = weight_ref.shape[2]
    value, down_t = unpacked(weight_ref)
    hidden = hidden_ref[:, value.shape[0] :]
    out_ref[:, :features] = before_ref[:, :features] + jnp.dot(hidden, value, preferred_element_type=F32)
    out_ref[:, features:] = before_ref[:, features:] + low_part(hidden, down_t)


def near_forward(mine, other, first, second):
    out = (mine.shape[0], 2 * first.shape[2] + LANES)
    return pl.pallas_call(
        near_kernel,
        in_specs=[vmem()] * 4,
        out_specs=[vmem()] * 2,
        out_shape=[jax.ShapeDtypeStruct(out, F32)] * 2,
        compiler_params=params(),
        name="near",
    )(mine, other, first, second)


def far_forward(hidden, weights, before):
    return pl.pallas_call(
        far_kernel,
        in_specs=[vmem()] * 3,
        out_specs=vmem(),
        out_shape=jax.ShapeDtypeStruct(before.shape, F32),
        compiler_params=params(),
        name="far",
    )(hidden, weights, before)


def plane_gather(w):
    return lax.all_to_all(jnp.broadcast_to(w[None], (X * Y,) + w.shape), XY, 0, 0)


def middle_kernel(mine_ref, other_ref, hidden_ref, read_ref, mask_ref, up_ref, out_ref):
    tokens, features = read_ref.shape
    rank = up_ref.shape[0] // 2
    base = mine_ref[:, :features] + other_ref[:, :features]
    low = mine_ref[:, features:] + other_ref[:, features:]
    low_b = low.astype(BF16)
    policy = base + ADAPTER_SCALE * jnp.dot(low_b, up_ref[...], preferred_element_type=F32)
    read = read_ref[...].astype(F32)
    sign = jnp.where(lax.broadcasted_iota(jnp.int32, (tokens, 1), 0) < tokens // 2, 1.0, -1.0)
    signed = mask_ref[...] * sign
    t_pol = jnp.tanh(policy)
    t_ref = jnp.tanh(base)
    scores = jnp.sum(read * (t_pol - t_ref), axis=1, keepdims=True) * signed
    total = jnp.sum(scores, axis=0, keepdims=True)
    grad = ((-DPO_BETA * signed) * read * (1.0 - t_pol * t_pol)).astype(BF16)
    low_grad_t = (
        ADAPTER_SCALE
        * lax.dot_general(up_ref[:rank, :], grad, (((1,), (1,)), ((), ())), preferred_element_type=F32)
    ).astype(BF16)
    twice = (low + pltpu.roll(low, rank, 1)).astype(BF16)
    up_grad = ADAPTER_SCALE * lax.dot_general(
        grad, twice, (((0,), (0,)), ((), ())), preferred_element_type=F32
    )
    wide = 2 * LANES
    part = features // (X * ZH * Y)
    lane = lax.broadcasted_iota(jnp.int32, (EXTRA, LANES), 1)
    sent = pieces(total, (EXTRA, LANES)).astype(BF16)
    for x in range(X):
        for y in range(Y):
            to = x * Y + y
            places = [(x * ZH + zh) * Y + y for zh in range(ZH)]
            for zh, s in enumerate(places):
                out_ref[to, zh * rank : (zh + 1) * rank, :] = jnp.dot(
                    low_grad_t, hidden_ref[:, s * wide : (s + 1) * wide], preferred_element_type=F32
                ).astype(BF16)
            both = jnp.where(
                lane < rank,
                up_grad[places[0] * part : (places[0] + 1) * part, :],
                up_grad[places[1] * part : (places[1] + 1) * part, :],
            )
            out_ref[to, ZH * rank :, :LANES] = both.astype(BF16)
            out_ref[to, ZH * rank :, LANES:] = sent


def plane_kernel(got_ref, out_ref):
    rank = (got_ref.shape[1] - EXTRA) // ZH
    rows = rank // ZL
    total = got_ref[0].astype(F32)
    for s in range(1, got_ref.shape[0]):
        total = total + got_ref[s].astype(F32)
    first = ZH * rank
    margin = jnp.sum(total[first : first + 1, LANES:], axis=1, keepdims=True)
    sent = pieces(margin, (8, LANES))
    lane = lax.broadcasted_iota(jnp.int32, (8, LANES), 1)
    upper = total[first : first + 8, :LANES]
    lower = total[first + 8 : first + 16, :LANES]
    packed = [
        jnp.where(lane < rank, upper, pltpu.roll(lower, rank, 1)),
        jnp.where(lane < rank, pltpu.roll(upper, rank, 1), lower),
    ]
    for zl in range(ZL):
        for zh in range(ZH):
            start = zh * rank + zl * rows
            tail = jnp.concatenate([packed[zh], sent], axis=1)
            out_ref[zl * ZH + zh] = jnp.concatenate(
                [total[start : start + rows, :], tail], axis=0
            ).astype(BF16)


def gate_kernel(got_ref, out_ref, diff_ref):
    total = None
    for zl in range(ZL):
        pair = got_ref[zl * ZH].astype(F32) + got_ref[zl * ZH + 1].astype(F32)
        diff = jnp.sum(pair[8:9, LANES:], axis=1, keepdims=True)
        gate = 1.0 / (1.0 + jnp.exp(DPO_BETA * diff))
        total = gate * pair if total is None else total + gate * pair
        diff_ref[zl : zl + 1, :] = jnp.broadcast_to(diff, (1, LANES))
    out_ref[...] = total


def shards(hidden_input, readout, response, value_matrix, adapter_down, adapter_up):
    seq_rows, width = hidden_input.shape[2:]
    tokens = 2 * seq_rows
    features = value_matrix.shape[1]
    rank = adapter_down.shape[1]
    core, zh, zl = lax.axis_index("core"), lax.axis_index("zh"), lax.axis_index("zl")
    hidden = hidden_input.reshape(tokens, width)

    value_half = lax.dynamic_slice_in_dim(value_matrix, core * LANES, LANES, 0)
    down_half = lax.dynamic_slice_in_dim(adapter_down, core * LANES, LANES, 0)
    packed = down_half.T.reshape(features // LANES, EXTRA, LANES).transpose(1, 0, 2).reshape(EXTRA, features)
    weights = jnp.concatenate([value_half, packed], axis=0)
    sizes = (ZL, 2, X, ZH, Y)
    axes = ("zl", "core", "x", "zh", "y")
    spots = list(np.ndindex(*sizes))
    flat = lambda p: int(np.ravel_multi_index(p, sizes))

    def along_z(step):
        moved = []
        for a, c, b, e, d in spots:
            z = (e * ZL + a + step) % (ZH * ZL)
            moved.append((flat((a, c, b, e, d)), flat((z % ZL, c, b, z // ZL, d))))
        return moved

    swap_core = [(0, 1), (1, 0)]
    odd = zl % 2
    half = features // 2

    weights_far = lax.ppermute(weights, axes, along_z(ZL))
    near = plane_gather(lax.dynamic_slice_in_dim(weights, odd * half, half, 1))
    mine, for_other = pl.pallas_call(
        order_kernel,
        in_specs=[pl.BlockSpec(memory_space=pltpu.SMEM), vmem()],
        out_specs=[vmem(), vmem()],
        out_shape=[jax.ShapeDtypeStruct((tokens, width // 2), BF16)] * 2,
        compiler_params=params(),
        name="order",
    )(jnp.stack([core, zh]).astype(jnp.int32), hidden)
    other = lax.ppermute(for_other, "core", swap_core)

    weights_far, near = lax.optimization_barrier((weights_far, near))
    far = plane_gather(weights_far)
    near_too = lax.ppermute(near, "zl", [(a, a ^ 1) for a in range(ZL)])
    near_mine, near_other = near_forward(
        mine, other, jnp.where(odd == 0, near, near_too), jnp.where(odd == 0, near_too, near)
    )
    part_other = far_forward(other, far, near_other)
    from_other = lax.ppermute(part_other, "core", swap_core)
    part_mine = far_forward(mine, far, near_mine)

    read = readout.reshape(tokens, features)
    mask = response.reshape(tokens, 1).astype(F32)
    up = jnp.pad(adapter_up, ((0, rank), (0, 0)))
    wide = width // (X * ZH * Y)
    sends = pl.pallas_call(
        middle_kernel,
        in_specs=[vmem()] * 6,
        out_specs=vmem(),
        out_shape=jax.ShapeDtypeStruct((X * Y, ZH * rank + EXTRA, wide), BF16),
        compiler_params=params(),
        name="middle",
    )(part_mine, from_other, hidden, read, mask, up)
    got = lax.all_to_all(sends, XY, 0, 0)
    along = pl.pallas_call(
        plane_kernel,
        in_specs=[vmem()],
        out_specs=vmem(),
        out_shape=jax.ShapeDtypeStruct((ZL * ZH, 16, wide), BF16),
        compiler_params=params(),
        name="plane",
    )(got)
    got = lax.all_to_all(along, ZZ, 0, 0)
    gated, diffs = pl.pallas_call(
        gate_kernel,
        in_specs=[vmem()],
        out_specs=[vmem(), vmem()],
        out_shape=[jax.ShapeDtypeStruct((16, wide), F32), jax.ShapeDtypeStruct((ZL, LANES), F32)],
        compiler_params=params(),
        name="gate",
    )(got)
    summed = lax.psum(gated, "core")
    rows = rank // ZL
    all_rows = lax.all_to_all(jnp.broadcast_to(summed[None, :rows], (ZL, rows, wide)), "zl", 0, 0)
    down_gradient = all_rows.reshape(rank, wide).T
    up_part = jnp.concatenate([summed[8:16, :rank], summed[8:16, rank : 2 * rank]], axis=0)
    margin = DPO_BETA * lax.dynamic_slice(diffs, (zl, 0), (1, 1)).reshape(1)
    return down_gradient, up_part, jax.nn.softplus(-margin), margin


def solution(mesh):
    fine = Mesh(np.asarray(mesh.devices).reshape(ZL, 2, X, ZH, Y), ("zl", "core", "x", "zh", "y"))
    dp, fsdp = ("zl", "core"), ("x", "zh", "y")
    placed = (
        P(dp, None, fsdp, None),
        P(dp, None, fsdp, None),
        P(dp, None, fsdp),
        P(fsdp, None),
        P(fsdp, None),
        P(),
    )
    return jax.shard_map(
        shards,
        mesh=fine,
        in_specs=placed,
        out_specs=(P(fsdp, None), P(fsdp, None), P(dp), P(dp)),
        check_vma=False,
    )
```

```python
import jax
import jax.numpy as jnp
import numpy as np
from jax import lax
from jax.experimental import pallas as pl
from jax.experimental.pallas import tpu as pltpu
from jax.sharding import Mesh, PartitionSpec as P

DPO_BETA = 0.5
ADAPTER_SCALE = 2.0
BF16 = jnp.bfloat16
F32 = jnp.float32
LANES = 128
X, Y, ZH, ZL = 4, 4, 2, 8
XY = ("x", "y")
ZZ = ("zl", "zh")
EXTRA = 16


def vmem():
    return pl.BlockSpec(memory_space=pltpu.VMEM)


def params():
    return pltpu.CompilerParams(vmem_limit_bytes=50 * 1024 * 1024)


def pieces(total, shape):
    full = jnp.broadcast_to(total, shape)
    high = full.astype(BF16).astype(F32)
    rest = full - high
    middle = rest.astype(BF16).astype(F32)
    low = rest - middle
    lane = lax.broadcasted_iota(jnp.int32, shape, 1)
    zero = jnp.zeros(shape, F32)
    return jnp.where(lane == 0, high, jnp.where(lane == 1, middle, jnp.where(lane == 2, low, zero)))


def anywhere():
    return pl.BlockSpec(memory_space=pl.ANY)


def fetches(where_ref, hidden_ref, buffer, sems, far):
    core = where_ref[0]
    zh = 1 - where_ref[1] if far else where_ref[1]
    copies = []
    for x in range(X):
        for y in range(Y):
            at = x * Y + y
            start = (((x * ZH + zh) * Y + y) * 2 + core) * LANES
            copies.append(
                pltpu.make_async_copy(
                    hidden_ref.at[:, pl.ds(pl.multiple_of(start, LANES), LANES)],
                    buffer.at[:, at * LANES : (at + 1) * LANES],
                    sems.at[at],
                )
            )
    return copies


def unpacked(weight_ref):
    sources, _, features = weight_ref.shape
    value = weight_ref[:, :LANES, :].reshape(sources * LANES, features)
    down_t = [
        jnp.concatenate([weight_ref[s, LANES:, g * LANES : (g + 1) * LANES] for s in range(sources)], axis=1)
        for g in range(features // LANES)
    ]
    return value, jnp.concatenate(down_t, axis=0)


def low_part(hidden, down_t):
    down_t = jnp.concatenate([down_t, jnp.zeros((LANES - down_t.shape[0], down_t.shape[1]), BF16)], axis=0)
    return lax.dot_general(hidden, down_t, (((1,), (1,)), ((), ())), preferred_element_type=F32)


def near_kernel(
    where_ref, mine_ref, other_ref, own_ref, passed_ref, out_mine_ref, out_other_ref, mine, other, mine_sems, other_sems
):
    copies = fetches(where_ref, mine_ref, mine, mine_sems, False)
    copies += fetches(where_ref, other_ref, other, other_sems, False)
    for copy in copies:
        copy.start()
    for copy in copies:
        copy.wait()

    def body(first_ref, second_ref):
        half = first_ref.shape[2]
        first, first_t = unpacked(first_ref)
        second, second_t = unpacked(second_ref)
        down_t = jnp.concatenate([first_t, second_t], axis=0)
        for ref, out_ref in ((mine, out_mine_ref), (other, out_other_ref)):
            hidden = ref[...]
            out_ref[:, :half] = jnp.dot(hidden, first, preferred_element_type=F32)
            out_ref[:, half : 2 * half] = jnp.dot(hidden, second, preferred_element_type=F32)
            out_ref[:, 2 * half :] = low_part(hidden, down_t)

    @pl.when(where_ref[2] == 0)
    def _():
        body(own_ref, passed_ref)

    @pl.when(where_ref[2] != 0)
    def _():
        body(passed_ref, own_ref)


def far_kernel(where_ref, hidden_ref, weight_ref, before_ref, out_ref, buffer, sems):
    copies = fetches(where_ref, hidden_ref, buffer, sems, True)
    for copy in copies:
        copy.start()
    features = weight_ref.shape[2]
    value, down_t = unpacked(weight_ref)
    for copy in copies:
        copy.wait()
    hidden = buffer[...]
    out_ref[:, :features] = before_ref[:, :features] + jnp.dot(hidden, value, preferred_element_type=F32)
    out_ref[:, features:] = before_ref[:, features:] + low_part(hidden, down_t)


def smem():
    return pl.BlockSpec(memory_space=pltpu.SMEM)


def near_forward(where, mine, other, own, passed):
    tokens, width = mine.shape
    out = (tokens, 2 * own.shape[2] + LANES)
    return pl.pallas_call(
        near_kernel,
        in_specs=[smem(), anywhere(), anywhere(), vmem(), vmem()],
        out_specs=[vmem()] * 2,
        out_shape=[jax.ShapeDtypeStruct(out, F32)] * 2,
        scratch_shapes=[pltpu.VMEM((tokens, width // 4), BF16)] * 2 + [pltpu.SemaphoreType.DMA((X * Y,))] * 2,
        compiler_params=params(),
        name="near",
    )(where, mine, other, own, passed)


def far_forward(where, hidden, weights, before):
    tokens, width = hidden.shape
    return pl.pallas_call(
        far_kernel,
        in_specs=[smem(), anywhere(), vmem(), vmem()],
        out_specs=vmem(),
        out_shape=jax.ShapeDtypeStruct(before.shape, F32),
        scratch_shapes=[pltpu.VMEM((tokens, width // 4), BF16), pltpu.SemaphoreType.DMA((X * Y,))],
        compiler_params=params(),
        name="far",
    )(where, hidden, weights, before)


def plane_gather(w):
    return lax.all_to_all(jnp.broadcast_to(w[None], (X * Y,) + w.shape), XY, 0, 0)


def middle_kernel(mine_ref, other_ref, held_ref, read_ref, mask_ref, up_ref, out_ref, hidden_ref, sem):
    copy = pltpu.make_async_copy(held_ref, hidden_ref, sem)
    copy.start()
    tokens, features = read_ref.shape
    rank = up_ref.shape[0] // 2
    base = mine_ref[:, :features] + other_ref[:, :features]
    low = mine_ref[:, features:] + other_ref[:, features:]
    low_b = low.astype(BF16)
    policy = base + ADAPTER_SCALE * jnp.dot(low_b, up_ref[...], preferred_element_type=F32)
    read = read_ref[...].astype(F32)
    sign = jnp.where(lax.broadcasted_iota(jnp.int32, (tokens, 1), 0) < tokens // 2, 1.0, -1.0)
    signed = mask_ref[...] * sign
    t_pol = jnp.tanh(policy)
    t_ref = jnp.tanh(base)
    scores = jnp.sum(read * (t_pol - t_ref), axis=1, keepdims=True) * signed
    total = jnp.sum(scores, axis=0, keepdims=True)
    grad = ((-DPO_BETA * signed) * read * (1.0 - t_pol * t_pol)).astype(BF16)
    low_grad_t = (
        ADAPTER_SCALE
        * lax.dot_general(up_ref[:rank, :], grad, (((1,), (1,)), ((), ())), preferred_element_type=F32)
    ).astype(BF16)
    twice = (low + pltpu.roll(low, rank, 1)).astype(BF16)
    up_grad = ADAPTER_SCALE * lax.dot_general(
        grad, twice, (((0,), (0,)), ((), ())), preferred_element_type=F32
    )
    wide = 2 * LANES
    part = features // (X * ZH * Y)
    lane = lax.broadcasted_iota(jnp.int32, (EXTRA, LANES), 1)
    sent = pieces(total, (EXTRA, LANES)).astype(BF16)
    copy.wait()
    for x in range(X):
        for y in range(Y):
            to = x * Y + y
            places = [(x * ZH + zh) * Y + y for zh in range(ZH)]
            for zh, s in enumerate(places):
                out_ref[to, zh * rank : (zh + 1) * rank, :] = jnp.dot(
                    low_grad_t, hidden_ref[:, s * wide : (s + 1) * wide], preferred_element_type=F32
                ).astype(BF16)
            both = jnp.where(
                lane < rank,
                up_grad[places[0] * part : (places[0] + 1) * part, :],
                up_grad[places[1] * part : (places[1] + 1) * part, :],
            )
            out_ref[to, ZH * rank :, :LANES] = both.astype(BF16)
            out_ref[to, ZH * rank :, LANES:] = sent


def plane_kernel(got_ref, out_ref):
    rank = (got_ref.shape[1] - EXTRA) // ZH
    rows = rank // ZL
    total = got_ref[0].astype(F32)
    for s in range(1, got_ref.shape[0]):
        total = total + got_ref[s].astype(F32)
    first = ZH * rank
    margin = jnp.sum(total[first : first + 1, LANES:], axis=1, keepdims=True)
    sent = pieces(margin, (8, LANES))
    lane = lax.broadcasted_iota(jnp.int32, (8, LANES), 1)
    upper = total[first : first + 8, :LANES]
    lower = total[first + 8 : first + 16, :LANES]
    packed = [
        jnp.where(lane < rank, upper, pltpu.roll(lower, rank, 1)),
        jnp.where(lane < rank, pltpu.roll(upper, rank, 1), lower),
    ]
    for zl in range(ZL):
        for zh in range(ZH):
            start = zh * rank + zl * rows
            tail = jnp.concatenate([packed[zh], sent], axis=1)
            out_ref[zl * ZH + zh] = jnp.concatenate(
                [total[start : start + rows, :], tail], axis=0
            ).astype(BF16)


def gate_kernel(got_ref, out_ref, diff_ref):
    total = None
    for zl in range(ZL):
        pair = got_ref[zl * ZH].astype(F32) + got_ref[zl * ZH + 1].astype(F32)
        diff = jnp.sum(pair[8:9, LANES:], axis=1, keepdims=True)
        gate = 1.0 / (1.0 + jnp.exp(DPO_BETA * diff))
        total = gate * pair if total is None else total + gate * pair
        diff_ref[zl : zl + 1, :] = jnp.broadcast_to(diff, (1, LANES))
    out_ref[...] = total


def shards(hidden_input, readout, response, value_matrix, adapter_down, adapter_up):
    seq_rows, width = hidden_input.shape[2:]
    tokens = 2 * seq_rows
    features = value_matrix.shape[1]
    rank = adapter_down.shape[1]
    core, zh, zl = lax.axis_index("core"), lax.axis_index("zh"), lax.axis_index("zl")
    hidden = hidden_input.reshape(tokens, width)

    value_half = lax.dynamic_slice_in_dim(value_matrix, core * LANES, LANES, 0)
    down_half = lax.dynamic_slice_in_dim(adapter_down, core * LANES, LANES, 0)
    packed = down_half.T.reshape(features // LANES, EXTRA, LANES).transpose(1, 0, 2).reshape(EXTRA, features)
    weights = jnp.concatenate([value_half, packed], axis=0)
    sizes = (ZL, 2, X, ZH, Y)
    axes = ("zl", "core", "x", "zh", "y")
    spots = list(np.ndindex(*sizes))
    flat = lambda p: int(np.ravel_multi_index(p, sizes))

    def along_z(step):
        moved = []
        for a, c, b, e, d in spots:
            z = (e * ZL + a + step) % (ZH * ZL)
            moved.append((flat((a, c, b, e, d)), flat((z % ZL, c, b, z // ZL, d))))
        return moved

    swap_core = [(0, 1), (1, 0)]
    odd = zl % 2
    half = features // 2

    weights_far = lax.ppermute(weights, axes, along_z(ZL))
    near = plane_gather(lax.dynamic_slice_in_dim(weights, odd * half, half, 1))
    where = jnp.stack([core, zh, odd]).astype(jnp.int32)
    other = lax.ppermute(hidden, "core", swap_core)

    weights_far, near = lax.optimization_barrier((weights_far, near))
    far = plane_gather(weights_far)
    passed = lax.ppermute(near, "zl", [(a, a ^ 1) for a in range(ZL)])
    near_mine, near_other = near_forward(where, hidden, other, near, passed)
    part_other = far_forward(where, other, far, near_other)
    from_other = lax.ppermute(part_other, "core", swap_core)
    part_mine = far_forward(where, hidden, far, near_mine)

    read = readout.reshape(tokens, features)
    mask = response.reshape(tokens, 1).astype(F32)
    up = jnp.pad(adapter_up, ((0, rank), (0, 0)))
    wide = width // (X * ZH * Y)
    sends = pl.pallas_call(
        middle_kernel,
        in_specs=[vmem(), vmem(), anywhere(), vmem(), vmem(), vmem()],
        out_specs=vmem(),
        out_shape=jax.ShapeDtypeStruct((X * Y, ZH * rank + EXTRA, wide), BF16),
        scratch_shapes=[pltpu.VMEM((tokens, width), BF16), pltpu.SemaphoreType.DMA],
        compiler_params=params(),
        name="middle",
    )(part_mine, from_other, hidden, read, mask, up)
    got = lax.all_to_all(sends, XY, 0, 0)
    along = pl.pallas_call(
        plane_kernel,
        in_specs=[vmem()],
        out_specs=vmem(),
        out_shape=jax.ShapeDtypeStruct((ZL * ZH, 16, wide), BF16),
        compiler_params=params(),
        name="plane",
    )(got)
    got = lax.all_to_all(along, ZZ, 0, 0)
    gated, diffs = pl.pallas_call(
        gate_kernel,
        in_specs=[vmem()],
        out_specs=[vmem(), vmem()],
        out_shape=[jax.ShapeDtypeStruct((16, wide), F32), jax.ShapeDtypeStruct((ZL, LANES), F32)],
        compiler_params=params(),
        name="gate",
    )(got)
    summed, diffs = lax.optimization_barrier((lax.psum(gated, "core"), diffs))
    rows = rank // ZL
    all_rows = lax.all_to_all(jnp.broadcast_to(summed[None, :rows], (ZL, rows, wide)), "zl", 0, 0)
    down_gradient = all_rows.reshape(rank, wide).T
    up_part = jnp.concatenate([summed[8:16, :rank], summed[8:16, rank : 2 * rank]], axis=0)
    margin = DPO_BETA * lax.dynamic_slice(diffs, (zl, 0), (1, 1)).reshape(1)
    return down_gradient, up_part, jax.nn.softplus(-margin), margin


def solution(mesh):
    fine = Mesh(np.asarray(mesh.devices).reshape(ZL, 2, X, ZH, Y), ("zl", "core", "x", "zh", "y"))
    dp, fsdp = ("zl", "core"), ("x", "zh", "y")
    placed = (
        P(dp, None, fsdp, None),
        P(dp, None, fsdp, None),
        P(dp, None, fsdp),
        P(fsdp, None),
        P(fsdp, None),
        P(),
    )
    return jax.shard_map(
        shards,
        mesh=fine,
        in_specs=placed,
        out_specs=(P(fsdp, None), P(fsdp, None), P(dp), P(dp)),
        check_vma=False,
    )
```

```python
import jax
import jax.numpy as jnp
import numpy as np
from jax import lax
from jax.experimental import pallas as pl
from jax.experimental.pallas import tpu as pltpu
from jax.sharding import Mesh, PartitionSpec as P

DPO_BETA = 0.5
ADAPTER_SCALE = 2.0
BF16 = jnp.bfloat16
F32 = jnp.float32
LANES = 128
X, Y, ZH, ZL = 4, 4, 2, 8
XY = ("x", "y")
ZZ = ("zl", "zh")
EXTRA = 16


def vmem():
    return pl.BlockSpec(memory_space=pltpu.VMEM)


def params(mib=50):
    return pltpu.CompilerParams(vmem_limit_bytes=mib * 1024 * 1024)


def pieces(total, shape):
    full = jnp.broadcast_to(total, shape)
    high = full.astype(BF16).astype(F32)
    rest = full - high
    middle = rest.astype(BF16).astype(F32)
    low = rest - middle
    lane = lax.broadcasted_iota(jnp.int32, shape, 1)
    zero = jnp.zeros(shape, F32)
    return jnp.where(lane == 0, high, jnp.where(lane == 1, middle, jnp.where(lane == 2, low, zero)))


def anywhere():
    return pl.BlockSpec(memory_space=pl.ANY)


def fetches(where_ref, hidden_ref, buffer, sems, far):
    core = where_ref[0]
    zh = 1 - where_ref[1] if far else where_ref[1]
    copies = []
    for x in range(X):
        for y in range(Y):
            at = x * Y + y
            start = (((x * ZH + zh) * Y + y) * 2 + core) * LANES
            copies.append(
                pltpu.make_async_copy(
                    hidden_ref.at[:, pl.ds(pl.multiple_of(start, LANES), LANES)],
                    buffer.at[:, at * LANES : (at + 1) * LANES],
                    sems.at[at],
                )
            )
    return copies


def unpacked(weight_ref):
    sources, _, features = weight_ref.shape
    value = weight_ref[:, :LANES, :].reshape(sources * LANES, features)
    down_t = [
        jnp.concatenate([weight_ref[s, LANES:, g * LANES : (g + 1) * LANES] for s in range(sources)], axis=1)
        for g in range(features // LANES)
    ]
    return value, jnp.concatenate(down_t, axis=0)


def low_part(hidden, down_t):
    down_t = jnp.concatenate([down_t, jnp.zeros((LANES - down_t.shape[0], down_t.shape[1]), BF16)], axis=0)
    return lax.dot_general(hidden, down_t, (((1,), (1,)), ((), ())), preferred_element_type=F32)


def own_kernel(where_ref, mine_ref, other_ref, own_ref, out_mine_ref, out_other_ref, mine, other, mine_sems, other_sems):
    copies = fetches(where_ref, mine_ref, mine, mine_sems, False)
    copies += fetches(where_ref, other_ref, other, other_sems, False)
    for copy in copies:
        copy.start()
    for copy in copies:
        copy.wait()
    half = own_ref.shape[2]
    value, down_t = unpacked(own_ref)
    nothing = jnp.zeros_like(down_t)

    def body(columns, rest, down_t):
        for ref, out_ref in ((mine, out_mine_ref), (other, out_other_ref)):
            hidden = ref[...]
            out_ref[:, columns] = jnp.dot(hidden, value, preferred_element_type=F32)
            out_ref[:, rest] = jnp.zeros((hidden.shape[0], half), F32)
            out_ref[:, 2 * half :] = low_part(hidden, down_t)

    @pl.when(where_ref[2] == 0)
    def _():
        body(slice(0, half), slice(half, 2 * half), jnp.concatenate([down_t, nothing], axis=0))

    @pl.when(where_ref[2] != 0)
    def _():
        body(slice(half, 2 * half), slice(0, half), jnp.concatenate([nothing, down_t], axis=0))


def last_kernel(keep, where_ref, hidden_ref, weight_ref, sent_ref, before_ref, out_ref, *refs):
    if keep:
        kept_ref, far, near, far_sems, near_sems, passed_ref, passed_sem, keep_sem = refs
    else:
        far, near, far_sems, near_sems, passed_ref, passed_sem = refs
    far_copies = fetches(where_ref, hidden_ref, far, far_sems, True)
    near_copies = fetches(where_ref, hidden_ref, near, near_sems, False)
    near_copies.append(pltpu.make_async_copy(sent_ref, passed_ref, passed_sem))
    for copy in far_copies + near_copies:
        copy.start()
    if keep:
        whole = pltpu.make_async_copy(hidden_ref, kept_ref, keep_sem)
        whole.start()
    features = weight_ref.shape[2]
    half = passed_ref.shape[2]
    value, down_t = unpacked(weight_ref)
    for copy in far_copies:
        copy.wait()
    hidden = far[...]
    out_ref[:, :features] = before_ref[:, :features] + jnp.dot(hidden, value, preferred_element_type=F32)
    out_ref[:, features:] = before_ref[:, features:] + low_part(hidden, down_t)
    for copy in near_copies:
        copy.wait()
    value, down_t = unpacked(passed_ref)
    nothing = jnp.zeros_like(down_t)

    def body(columns, down_t):
        hidden = near[...]
        out_ref[:, columns] += jnp.dot(hidden, value, preferred_element_type=F32)
        out_ref[:, features:] += low_part(hidden, down_t)

    @pl.when(where_ref[2] == 0)
    def _():
        body(slice(half, features), jnp.concatenate([nothing, down_t], axis=0))

    @pl.when(where_ref[2] != 0)
    def _():
        body(slice(0, half), jnp.concatenate([down_t, nothing], axis=0))

    if keep:
        whole.wait()


def smem():
    return pl.BlockSpec(memory_space=pltpu.SMEM)


def blocks(tokens, width, count):
    return [pltpu.VMEM((tokens, width // 4), BF16)] * count + [pltpu.SemaphoreType.DMA((X * Y,))] * count


def own_forward(where, mine, other, own):
    tokens, width = mine.shape
    out = (tokens, 2 * own.shape[2] + LANES)
    return pl.pallas_call(
        own_kernel,
        in_specs=[smem(), anywhere(), anywhere(), vmem()],
        out_specs=[vmem()] * 2,
        out_shape=[jax.ShapeDtypeStruct(out, F32)] * 2,
        scratch_shapes=blocks(tokens, width, 2),
        compiler_params=params(),
        name="own",
    )(where, mine, other, own)


def last_forward(where, hidden, weights, passed, before, keep):
    tokens, width = hidden.shape
    out = jax.ShapeDtypeStruct(before.shape, F32)
    scratch = blocks(tokens, width, 2) + [pltpu.VMEM(passed.shape, BF16), pltpu.SemaphoreType.DMA]
    return pl.pallas_call(
        lambda *refs: last_kernel(keep, *refs),
        in_specs=[smem(), anywhere(), vmem(), anywhere(), vmem()],
        out_specs=[vmem(), vmem()] if keep else vmem(),
        out_shape=[out, jax.ShapeDtypeStruct(hidden.shape, BF16)] if keep else out,
        scratch_shapes=scratch + [pltpu.SemaphoreType.DMA] if keep else scratch,
        compiler_params=params(48),
        name="last",
    )(where, hidden, weights, passed, before)


def plane_gather(w):
    return lax.all_to_all(jnp.broadcast_to(w[None], (X * Y,) + w.shape), XY, 0, 0)


def middle_kernel(mine_ref, other_ref, hidden_ref, read_ref, mask_ref, up_ref, out_ref):
    tokens, features = read_ref.shape
    rank = up_ref.shape[0] // 2
    base = mine_ref[:, :features] + other_ref[:, :features]
    low = mine_ref[:, features:] + other_ref[:, features:]
    low_b = low.astype(BF16)
    policy = base + ADAPTER_SCALE * jnp.dot(low_b, up_ref[...], preferred_element_type=F32)
    read = read_ref[...].astype(F32)
    sign = jnp.where(lax.broadcasted_iota(jnp.int32, (tokens, 1), 0) < tokens // 2, 1.0, -1.0)
    signed = mask_ref[...] * sign
    t_pol = jnp.tanh(policy)
    t_ref = jnp.tanh(base)
    scores = jnp.sum(read * (t_pol - t_ref), axis=1, keepdims=True) * signed
    total = jnp.sum(scores, axis=0, keepdims=True)
    grad = ((-DPO_BETA * signed) * read * (1.0 - t_pol * t_pol)).astype(BF16)
    low_grad_t = (
        ADAPTER_SCALE
        * lax.dot_general(up_ref[:rank, :], grad, (((1,), (1,)), ((), ())), preferred_element_type=F32)
    ).astype(BF16)
    twice = (low + pltpu.roll(low, rank, 1)).astype(BF16)
    up_grad = ADAPTER_SCALE * lax.dot_general(
        grad, twice, (((0,), (0,)), ((), ())), preferred_element_type=F32
    )
    wide = 2 * LANES
    part = features // (X * ZH * Y)
    lane = lax.broadcasted_iota(jnp.int32, (EXTRA, LANES), 1)
    sent = pieces(total, (EXTRA, LANES)).astype(BF16)
    for x in range(X):
        for y in range(Y):
            to = x * Y + y
            places = [(x * ZH + zh) * Y + y for zh in range(ZH)]
            for zh, s in enumerate(places):
                out_ref[to, zh * rank : (zh + 1) * rank, :] = jnp.dot(
                    low_grad_t, hidden_ref[:, s * wide : (s + 1) * wide], preferred_element_type=F32
                ).astype(BF16)
            both = jnp.where(
                lane < rank,
                up_grad[places[0] * part : (places[0] + 1) * part, :],
                up_grad[places[1] * part : (places[1] + 1) * part, :],
            )
            out_ref[to, ZH * rank :, :LANES] = both.astype(BF16)
            out_ref[to, ZH * rank :, LANES:] = sent


def plane_kernel(got_ref, out_ref):
    rank = (got_ref.shape[1] - EXTRA) // ZH
    rows = rank // ZL
    total = got_ref[0].astype(F32)
    for s in range(1, got_ref.shape[0]):
        total = total + got_ref[s].astype(F32)
    first = ZH * rank
    margin = jnp.sum(total[first : first + 1, LANES:], axis=1, keepdims=True)
    sent = pieces(margin, (8, LANES))
    lane = lax.broadcasted_iota(jnp.int32, (8, LANES), 1)
    upper = total[first : first + 8, :LANES]
    lower = total[first + 8 : first + 16, :LANES]
    packed = [
        jnp.where(lane < rank, upper, pltpu.roll(lower, rank, 1)),
        jnp.where(lane < rank, pltpu.roll(upper, rank, 1), lower),
    ]
    for zl in range(ZL):
        for zh in range(ZH):
            start = zh * rank + zl * rows
            tail = jnp.concatenate([packed[zh], sent], axis=1)
            out_ref[zl * ZH + zh] = jnp.concatenate(
                [total[start : start + rows, :], tail], axis=0
            ).astype(BF16)


def gate_kernel(got_ref, out_ref, diff_ref):
    total = None
    for zl in range(ZL):
        pair = got_ref[zl * ZH].astype(F32) + got_ref[zl * ZH + 1].astype(F32)
        diff = jnp.sum(pair[8:9, LANES:], axis=1, keepdims=True)
        gate = 1.0 / (1.0 + jnp.exp(DPO_BETA * diff))
        total = gate * pair if total is None else total + gate * pair
        diff_ref[zl : zl + 1, :] = jnp.broadcast_to(diff, (1, LANES))
    out_ref[...] = total


def shards(hidden_input, readout, response, value_matrix, adapter_down, adapter_up):
    seq_rows, width = hidden_input.shape[2:]
    tokens = 2 * seq_rows
    features = value_matrix.shape[1]
    rank = adapter_down.shape[1]
    core, zh, zl = lax.axis_index("core"), lax.axis_index("zh"), lax.axis_index("zl")
    hidden = hidden_input.reshape(tokens, width)

    value_half = lax.dynamic_slice_in_dim(value_matrix, core * LANES, LANES, 0)
    down_half = lax.dynamic_slice_in_dim(adapter_down, core * LANES, LANES, 0)
    packed = down_half.T.reshape(features // LANES, EXTRA, LANES).transpose(1, 0, 2).reshape(EXTRA, features)
    weights = jnp.concatenate([value_half, packed], axis=0)
    sizes = (ZL, 2, X, ZH, Y)
    axes = ("zl", "core", "x", "zh", "y")
    spots = list(np.ndindex(*sizes))
    flat = lambda p: int(np.ravel_multi_index(p, sizes))

    mirror = [(flat((a, c, b, e, d)), flat((ZL - 1 - a, c, b, 1 - e, d))) for a, c, b, e, d in spots]
    swap_core = [(0, 1), (1, 0)]
    odd = zl % 2
    half = features // 2

    weights_far = lax.ppermute(weights, axes, mirror)
    near = plane_gather(lax.dynamic_slice_in_dim(weights, odd * half, half, 1))
    where = jnp.stack([core, zh, odd]).astype(jnp.int32)
    other = lax.ppermute(hidden, "core", swap_core)

    weights_far, near = lax.optimization_barrier((weights_far, near))
    far = plane_gather(weights_far)
    passed = lax.ppermute(near, "zl", [(a, a ^ 1) for a in range(ZL)])
    before_mine, before_other = own_forward(where, hidden, other, near)
    part_other = last_forward(where, other, far, passed, before_other, False)
    from_other = lax.ppermute(part_other, "core", swap_core)
    part_mine, kept = last_forward(where, hidden, far, passed, before_mine, True)

    read = readout.reshape(tokens, features)
    mask = response.reshape(tokens, 1).astype(F32)
    up = jnp.pad(adapter_up, ((0, rank), (0, 0)))
    wide = width // (X * ZH * Y)
    sends = pl.pallas_call(
        middle_kernel,
        in_specs=[vmem()] * 6,
        out_specs=vmem(),
        out_shape=jax.ShapeDtypeStruct((X * Y, ZH * rank + EXTRA, wide), BF16),
        compiler_params=params(),
        name="middle",
    )(part_mine, from_other, kept, read, mask, up)
    got = lax.all_to_all(sends, XY, 0, 0)
    along = pl.pallas_call(
        plane_kernel,
        in_specs=[vmem()],
        out_specs=vmem(),
        out_shape=jax.ShapeDtypeStruct((ZL * ZH, 16, wide), BF16),
        compiler_params=params(),
        name="plane",
    )(got)
    got = lax.all_to_all(along, ZZ, 0, 0)
    gated, diffs = pl.pallas_call(
        gate_kernel,
        in_specs=[vmem()],
        out_specs=[vmem(), vmem()],
        out_shape=[jax.ShapeDtypeStruct((16, wide), F32), jax.ShapeDtypeStruct((ZL, LANES), F32)],
        compiler_params=params(),
        name="gate",
    )(got)
    summed, diffs = lax.optimization_barrier((lax.psum(gated, "core"), diffs))
    rows = rank // ZL
    all_rows = lax.all_to_all(jnp.broadcast_to(summed[None, :rows], (ZL, rows, wide)), "zl", 0, 0)
    down_gradient = all_rows.reshape(rank, wide).T
    up_part = jnp.concatenate([summed[8:16, :rank], summed[8:16, rank : 2 * rank]], axis=0)
    margin = DPO_BETA * lax.dynamic_slice(diffs, (zl, 0), (1, 1)).reshape(1)
    return down_gradient, up_part, jax.nn.softplus(-margin), margin


def solution(mesh):
    fine = Mesh(np.asarray(mesh.devices).reshape(ZL, 2, X, ZH, Y), ("zl", "core", "x", "zh", "y"))
    dp, fsdp = ("zl", "core"), ("x", "zh", "y")
    placed = (
        P(dp, None, fsdp, None),
        P(dp, None, fsdp, None),
        P(dp, None, fsdp),
        P(fsdp, None),
        P(fsdp, None),
        P(),
    )
    return jax.shard_map(
        shards,
        mesh=fine,
        in_specs=placed,
        out_specs=(P(fsdp, None), P(fsdp, None), P(dp), P(dp)),
        check_vma=False,
    )
```

```python
import jax
import jax.numpy as jnp
import numpy as np
from jax import lax
from jax.experimental import pallas as pl
from jax.experimental.pallas import tpu as pltpu
from jax.sharding import Mesh, PartitionSpec as P

DPO_BETA = 0.5
ADAPTER_SCALE = 2.0
BF16 = jnp.bfloat16
F32 = jnp.float32
LANES = 128
X, Y, ZH, ZL = 4, 4, 2, 8
XY = ("x", "y")
ZZ = ("zl", "zh")
EXTRA = 16
OWN, LAST, MIDDLE = 50, 20, 20


def vmem():
    return pl.BlockSpec(memory_space=pltpu.VMEM)


def params(mib=50):
    return pltpu.CompilerParams(vmem_limit_bytes=mib * 1024 * 1024)


def pieces(total, shape):
    full = jnp.broadcast_to(total, shape)
    high = full.astype(BF16).astype(F32)
    rest = full - high
    middle = rest.astype(BF16).astype(F32)
    low = rest - middle
    lane = lax.broadcasted_iota(jnp.int32, shape, 1)
    zero = jnp.zeros(shape, F32)
    return jnp.where(lane == 0, high, jnp.where(lane == 1, middle, jnp.where(lane == 2, low, zero)))


def anywhere():
    return pl.BlockSpec(memory_space=pl.ANY)


def fetches(where_ref, hidden_ref, buffer, sems, far):
    core = where_ref[0]
    zh = 1 - where_ref[1] if far else where_ref[1]
    copies = []
    for x in range(X):
        for y in range(Y):
            at = x * Y + y
            start = (((x * ZH + zh) * Y + y) * 2 + core) * LANES
            copies.append(
                pltpu.make_async_copy(
                    hidden_ref.at[:, pl.ds(pl.multiple_of(start, LANES), LANES)],
                    buffer.at[:, at * LANES : (at + 1) * LANES],
                    sems.at[at],
                )
            )
    return copies


def unpacked(weight_ref):
    sources, _, features = weight_ref.shape
    value = weight_ref[:, :LANES, :].reshape(sources * LANES, features)
    down_t = [
        jnp.concatenate([weight_ref[s, LANES:, g * LANES : (g + 1) * LANES] for s in range(sources)], axis=1)
        for g in range(features // LANES)
    ]
    return value, jnp.concatenate(down_t, axis=0)


def low_part(hidden, down_t):
    down_t = jnp.concatenate([down_t, jnp.zeros((LANES - down_t.shape[0], down_t.shape[1]), BF16)], axis=0)
    return lax.dot_general(hidden, down_t, (((1,), (1,)), ((), ())), preferred_element_type=F32)


def own_kernel(where_ref, mine_ref, other_ref, own_ref, *refs):
    out_mine_ref, out_other_ref, near_mine, near_other, far_mine, far_other, sems = refs
    held = ((mine_ref, near_mine, False), (other_ref, near_other, False), (mine_ref, far_mine, True), (other_ref, far_other, True))
    copies = [
        copy
        for at, (ref, block_ref, far) in enumerate(held)
        for copy in fetches(where_ref, ref, block_ref, sems.at[at], far)
    ]
    for copy in copies:
        copy.start()
    for copy in copies:
        copy.wait()
    half = own_ref.shape[2]
    value, down_t = unpacked(own_ref)
    nothing = jnp.zeros_like(down_t)

    def body(columns, rest, down_t):
        for ref, out_ref in ((near_mine, out_mine_ref), (near_other, out_other_ref)):
            hidden = ref[...]
            out_ref[:, columns] = jnp.dot(hidden, value, preferred_element_type=F32)
            out_ref[:, rest] = jnp.zeros((hidden.shape[0], half), F32)
            out_ref[:, 2 * half :] = low_part(hidden, down_t)

    @pl.when(where_ref[2] == 0)
    def _():
        body(slice(0, half), slice(half, 2 * half), jnp.concatenate([down_t, nothing], axis=0))

    @pl.when(where_ref[2] != 0)
    def _():
        body(slice(half, 2 * half), slice(0, half), jnp.concatenate([nothing, down_t], axis=0))


def last_kernel(where_ref, near_ref, far_ref, weight_ref, passed_ref, before_ref, out_ref):
    features = weight_ref.shape[2]
    half = passed_ref.shape[2]
    value, down_t = unpacked(weight_ref)
    far = far_ref[...]
    out_ref[:, :features] = before_ref[:, :features] + jnp.dot(far, value, preferred_element_type=F32)
    out_ref[:, features:] = before_ref[:, features:] + low_part(far, down_t)
    value, down_t = unpacked(passed_ref)
    nothing = jnp.zeros_like(down_t)

    def body(columns, down_t):
        near = near_ref[...]
        out_ref[:, columns] += jnp.dot(near, value, preferred_element_type=F32)
        out_ref[:, features:] += low_part(near, down_t)

    @pl.when(where_ref[2] == 0)
    def _():
        body(slice(half, features), jnp.concatenate([nothing, down_t], axis=0))

    @pl.when(where_ref[2] != 0)
    def _():
        body(slice(0, half), jnp.concatenate([down_t, nothing], axis=0))


def smem():
    return pl.BlockSpec(memory_space=pltpu.SMEM)


def own_forward(where, mine, other, own):
    tokens, width = mine.shape
    out = jax.ShapeDtypeStruct((tokens, 2 * own.shape[2] + LANES), F32)
    block = jax.ShapeDtypeStruct((tokens, width // 4), BF16)
    return pl.pallas_call(
        own_kernel,
        in_specs=[smem(), anywhere(), anywhere(), vmem()],
        out_specs=[vmem()] * 6,
        out_shape=[out] * 2 + [block] * 4,
        scratch_shapes=[pltpu.SemaphoreType.DMA((4, X * Y))],
        compiler_params=params(OWN),
        name="own",
    )(where, mine, other, own)


def last_forward(where, near, far, weights, passed, before):
    return pl.pallas_call(
        last_kernel,
        in_specs=[smem()] + [vmem()] * 5,
        out_specs=vmem(),
        out_shape=jax.ShapeDtypeStruct(before.shape, F32),
        compiler_params=params(LAST),
        name="last",
    )(where, near, far, weights, passed, before)


def plane_gather(w):
    return lax.all_to_all(jnp.broadcast_to(w[None], (X * Y,) + w.shape), XY, 0, 0)


def middle_kernel(mine_ref, other_ref, hidden_ref, read_ref, mask_ref, up_ref, out_ref):
    tokens, features = read_ref.shape
    rank = up_ref.shape[0] // 2
    base = mine_ref[:, :features] + other_ref[:, :features]
    low = mine_ref[:, features:] + other_ref[:, features:]
    low_b = low.astype(BF16)
    policy = base + ADAPTER_SCALE * jnp.dot(low_b, up_ref[...], preferred_element_type=F32)
    read = read_ref[...].astype(F32)
    sign = jnp.where(lax.broadcasted_iota(jnp.int32, (tokens, 1), 0) < tokens // 2, 1.0, -1.0)
    signed = mask_ref[...] * sign
    t_pol = jnp.tanh(policy)
    t_ref = jnp.tanh(base)
    scores = jnp.sum(read * (t_pol - t_ref), axis=1, keepdims=True) * signed
    total = jnp.sum(scores, axis=0, keepdims=True)
    grad = ((-DPO_BETA * signed) * read * (1.0 - t_pol * t_pol)).astype(BF16)
    low_grad_t = (
        ADAPTER_SCALE
        * lax.dot_general(up_ref[:rank, :], grad, (((1,), (1,)), ((), ())), preferred_element_type=F32)
    ).astype(BF16)
    twice = (low + pltpu.roll(low, rank, 1)).astype(BF16)
    up_grad = ADAPTER_SCALE * lax.dot_general(
        grad, twice, (((0,), (0,)), ((), ())), preferred_element_type=F32
    )
    wide = 2 * LANES
    part = features // (X * ZH * Y)
    lane = lax.broadcasted_iota(jnp.int32, (EXTRA, LANES), 1)
    sent = pieces(total, (EXTRA, LANES)).astype(BF16)
    for x in range(X):
        for y in range(Y):
            to = x * Y + y
            places = [(x * ZH + zh) * Y + y for zh in range(ZH)]
            for zh, s in enumerate(places):
                out_ref[to, zh * rank : (zh + 1) * rank, :] = jnp.dot(
                    low_grad_t, hidden_ref[:, s * wide : (s + 1) * wide], preferred_element_type=F32
                ).astype(BF16)
            both = jnp.where(
                lane < rank,
                up_grad[places[0] * part : (places[0] + 1) * part, :],
                up_grad[places[1] * part : (places[1] + 1) * part, :],
            )
            out_ref[to, ZH * rank :, :LANES] = both.astype(BF16)
            out_ref[to, ZH * rank :, LANES:] = sent


def plane_kernel(got_ref, out_ref):
    rank = (got_ref.shape[1] - EXTRA) // ZH
    rows = rank // ZL
    total = got_ref[0].astype(F32)
    for s in range(1, got_ref.shape[0]):
        total = total + got_ref[s].astype(F32)
    first = ZH * rank
    margin = jnp.sum(total[first : first + 1, LANES:], axis=1, keepdims=True)
    sent = pieces(margin, (8, LANES))
    lane = lax.broadcasted_iota(jnp.int32, (8, LANES), 1)
    upper = total[first : first + 8, :LANES]
    lower = total[first + 8 : first + 16, :LANES]
    packed = [
        jnp.where(lane < rank, upper, pltpu.roll(lower, rank, 1)),
        jnp.where(lane < rank, pltpu.roll(upper, rank, 1), lower),
    ]
    for zl in range(ZL):
        for zh in range(ZH):
            start = zh * rank + zl * rows
            tail = jnp.concatenate([packed[zh], sent], axis=1)
            out_ref[zl * ZH + zh] = jnp.concatenate(
                [total[start : start + rows, :], tail], axis=0
            ).astype(BF16)


def gate_kernel(got_ref, out_ref, diff_ref):
    total = None
    for zl in range(ZL):
        pair = got_ref[zl * ZH].astype(F32) + got_ref[zl * ZH + 1].astype(F32)
        diff = jnp.sum(pair[8:9, LANES:], axis=1, keepdims=True)
        gate = 1.0 / (1.0 + jnp.exp(DPO_BETA * diff))
        total = gate * pair if total is None else total + gate * pair
        diff_ref[zl : zl + 1, :] = jnp.broadcast_to(diff, (1, LANES))
    out_ref[...] = total


def shards(hidden_input, readout, response, value_matrix, adapter_down, adapter_up):
    seq_rows, width = hidden_input.shape[2:]
    tokens = 2 * seq_rows
    features = value_matrix.shape[1]
    rank = adapter_down.shape[1]
    core, zh, zl = lax.axis_index("core"), lax.axis_index("zh"), lax.axis_index("zl")
    hidden = hidden_input.reshape(tokens, width)

    value_half = lax.dynamic_slice_in_dim(value_matrix, core * LANES, LANES, 0)
    down_half = lax.dynamic_slice_in_dim(adapter_down, core * LANES, LANES, 0)
    packed = down_half.T.reshape(features // LANES, EXTRA, LANES).transpose(1, 0, 2).reshape(EXTRA, features)
    weights = jnp.concatenate([value_half, packed], axis=0)
    sizes = (ZL, 2, X, ZH, Y)
    axes = ("zl", "core", "x", "zh", "y")
    spots = list(np.ndindex(*sizes))
    flat = lambda p: int(np.ravel_multi_index(p, sizes))

    mirror = [(flat((a, c, b, e, d)), flat((ZL - 1 - a, c, b, 1 - e, d))) for a, c, b, e, d in spots]
    swap_core = [(0, 1), (1, 0)]
    odd = zl % 2
    half = features // 2

    weights_far = lax.ppermute(weights, axes, mirror)
    near = plane_gather(lax.dynamic_slice_in_dim(weights, odd * half, half, 1))
    where = jnp.stack([core, zh, odd]).astype(jnp.int32)
    other = lax.ppermute(hidden, "core", swap_core)

    weights_far, near = lax.optimization_barrier((weights_far, near))
    far = plane_gather(weights_far)
    passed = lax.ppermute(near, "zl", [(a, a ^ 1) for a in range(ZL)])
    before_mine, before_other, near_mine, near_other, far_mine, far_other = own_forward(where, hidden, other, near)
    part_other = last_forward(where, near_other, far_other, far, passed, before_other)
    from_other = lax.ppermute(part_other, "core", swap_core)
    part_mine = last_forward(where, near_mine, far_mine, far, passed, before_mine)

    read = readout.reshape(tokens, features)
    mask = response.reshape(tokens, 1).astype(F32)
    up = jnp.pad(adapter_up, ((0, rank), (0, 0)))
    wide = width // (X * ZH * Y)
    sends = pl.pallas_call(
        middle_kernel,
        in_specs=[vmem()] * 6,
        out_specs=vmem(),
        out_shape=jax.ShapeDtypeStruct((X * Y, ZH * rank + EXTRA, wide), BF16),
        compiler_params=params(MIDDLE),
        name="middle",
    )(part_mine, from_other, hidden, read, mask, up)
    got = lax.all_to_all(sends, XY, 0, 0)
    along = pl.pallas_call(
        plane_kernel,
        in_specs=[vmem()],
        out_specs=vmem(),
        out_shape=jax.ShapeDtypeStruct((ZL * ZH, 16, wide), BF16),
        compiler_params=params(),
        name="plane",
    )(got)
    got = lax.all_to_all(along, ZZ, 0, 0)
    gated, diffs = pl.pallas_call(
        gate_kernel,
        in_specs=[vmem()],
        out_specs=[vmem(), vmem()],
        out_shape=[jax.ShapeDtypeStruct((16, wide), F32), jax.ShapeDtypeStruct((ZL, LANES), F32)],
        compiler_params=params(),
        name="gate",
    )(got)
    summed, diffs = lax.optimization_barrier((lax.psum(gated, "core"), diffs))
    rows = rank // ZL
    all_rows = lax.all_to_all(jnp.broadcast_to(summed[None, :rows], (ZL, rows, wide)), "zl", 0, 0)
    down_gradient = all_rows.reshape(rank, wide).T
    up_part = jnp.concatenate([summed[8:16, :rank], summed[8:16, rank : 2 * rank]], axis=0)
    margin = DPO_BETA * lax.dynamic_slice(diffs, (zl, 0), (1, 1)).reshape(1)
    return down_gradient, up_part, jax.nn.softplus(-margin), margin


def solution(mesh):
    fine = Mesh(np.asarray(mesh.devices).reshape(ZL, 2, X, ZH, Y), ("zl", "core", "x", "zh", "y"))
    dp, fsdp = ("zl", "core"), ("x", "zh", "y")
    placed = (
        P(dp, None, fsdp, None),
        P(dp, None, fsdp, None),
        P(dp, None, fsdp),
        P(fsdp, None),
        P(fsdp, None),
        P(),
    )
    return jax.shard_map(
        shards,
        mesh=fine,
        in_specs=placed,
        out_specs=(P(fsdp, None), P(fsdp, None), P(dp), P(dp)),
        check_vma=False,
    )
```

```python
import jax
import jax.numpy as jnp
import numpy as np
from jax import lax
from jax.experimental import pallas as pl
from jax.experimental.pallas import tpu as pltpu
from jax.sharding import Mesh, PartitionSpec as P

DPO_BETA = 0.5
ADAPTER_SCALE = 2.0
BF16 = jnp.bfloat16
F32 = jnp.float32
LANES = 128
X, Y, ZH, ZL = 4, 4, 2, 8
XY = ("x", "y")
ZZ = ("zl", "zh")
EXTRA = 16
OWN, PASSED, LAST, MIDDLE = 50, 20, 20, 20


def vmem():
    return pl.BlockSpec(memory_space=pltpu.VMEM)


def params(mib=50):
    return pltpu.CompilerParams(vmem_limit_bytes=mib * 1024 * 1024)


def pieces(total, shape):
    full = jnp.broadcast_to(total, shape)
    high = full.astype(BF16).astype(F32)
    rest = full - high
    middle = rest.astype(BF16).astype(F32)
    low = rest - middle
    lane = lax.broadcasted_iota(jnp.int32, shape, 1)
    zero = jnp.zeros(shape, F32)
    return jnp.where(lane == 0, high, jnp.where(lane == 1, middle, jnp.where(lane == 2, low, zero)))


def anywhere():
    return pl.BlockSpec(memory_space=pl.ANY)


def fetches(where_ref, hidden_ref, buffer, sems, far):
    core = where_ref[0]
    zh = 1 - where_ref[1] if far else where_ref[1]
    copies = []
    for x in range(X):
        for y in range(Y):
            at = x * Y + y
            start = (((x * ZH + zh) * Y + y) * 2 + core) * LANES
            copies.append(
                pltpu.make_async_copy(
                    hidden_ref.at[:, pl.ds(pl.multiple_of(start, LANES), LANES)],
                    buffer.at[:, at * LANES : (at + 1) * LANES],
                    sems.at[at],
                )
            )
    return copies


def unpacked(weight_ref):
    sources, _, features = weight_ref.shape
    value = weight_ref[:, :LANES, :].reshape(sources * LANES, features)
    down_t = [
        jnp.concatenate([weight_ref[s, LANES:, g * LANES : (g + 1) * LANES] for s in range(sources)], axis=1)
        for g in range(features // LANES)
    ]
    return value, jnp.concatenate(down_t, axis=0)


def low_part(hidden, down_t):
    down_t = jnp.concatenate([down_t, jnp.zeros((LANES - down_t.shape[0], down_t.shape[1]), BF16)], axis=0)
    return lax.dot_general(hidden, down_t, (((1,), (1,)), ((), ())), preferred_element_type=F32)


def own_kernel(where_ref, mine_ref, other_ref, own_ref, *refs):
    out_mine_ref, out_other_ref, near_mine, near_other, far_mine, far_other, sems = refs
    held = ((mine_ref, near_mine, False), (other_ref, near_other, False), (mine_ref, far_mine, True), (other_ref, far_other, True))
    copies = [
        copy
        for at, (ref, block_ref, far) in enumerate(held)
        for copy in fetches(where_ref, ref, block_ref, sems.at[at], far)
    ]
    for copy in copies:
        copy.start()
    for copy in copies:
        copy.wait()
    half = own_ref.shape[2]
    value, down_t = unpacked(own_ref)
    nothing = jnp.zeros_like(down_t)

    def body(columns, rest, down_t):
        for ref, out_ref in ((near_mine, out_mine_ref), (near_other, out_other_ref)):
            hidden = ref[...]
            out_ref[:, columns] = jnp.dot(hidden, value, preferred_element_type=F32)
            out_ref[:, rest] = jnp.zeros((hidden.shape[0], half), F32)
            out_ref[:, 2 * half :] = low_part(hidden, down_t)

    @pl.when(where_ref[2] == 0)
    def _():
        body(slice(0, half), slice(half, 2 * half), jnp.concatenate([down_t, nothing], axis=0))

    @pl.when(where_ref[2] != 0)
    def _():
        body(slice(half, 2 * half), slice(0, half), jnp.concatenate([nothing, down_t], axis=0))


def passed_kernel(where_ref, mine_ref, other_ref, passed_ref, old_mine_ref, old_other_ref, new_mine_ref, new_other_ref):
    half = passed_ref.shape[2]
    value, down_t = unpacked(passed_ref)
    nothing = jnp.zeros_like(down_t)

    def body(columns, rest, down_t):
        for near_ref, old_ref, new_ref in (
            (mine_ref, old_mine_ref, new_mine_ref),
            (other_ref, old_other_ref, new_other_ref),
        ):
            near = near_ref[...]
            new_ref[:, columns] = old_ref[:, columns] + jnp.dot(near, value, preferred_element_type=F32)
            new_ref[:, rest] = old_ref[:, rest]
            new_ref[:, 2 * half :] = old_ref[:, 2 * half :] + low_part(near, down_t)

    @pl.when(where_ref[2] == 0)
    def _():
        body(slice(half, 2 * half), slice(0, half), jnp.concatenate([nothing, down_t], axis=0))

    @pl.when(where_ref[2] != 0)
    def _():
        body(slice(0, half), slice(half, 2 * half), jnp.concatenate([down_t, nothing], axis=0))


def last_kernel(far_ref, weight_ref, before_ref, out_ref):
    features = weight_ref.shape[2]
    value, down_t = unpacked(weight_ref)
    far = far_ref[...]
    out_ref[:, :features] = before_ref[:, :features] + jnp.dot(far, value, preferred_element_type=F32)
    out_ref[:, features:] = before_ref[:, features:] + low_part(far, down_t)


def smem():
    return pl.BlockSpec(memory_space=pltpu.SMEM)


def own_forward(where, mine, other, own):
    tokens, width = mine.shape
    out = jax.ShapeDtypeStruct((tokens, 2 * own.shape[2] + LANES), F32)
    block = jax.ShapeDtypeStruct((tokens, width // 4), BF16)
    return pl.pallas_call(
        own_kernel,
        in_specs=[smem(), anywhere(), anywhere(), vmem()],
        out_specs=[vmem()] * 6,
        out_shape=[out] * 2 + [block] * 4,
        scratch_shapes=[pltpu.SemaphoreType.DMA((4, X * Y))],
        compiler_params=params(OWN),
        name="own",
    )(where, mine, other, own)


def passed_forward(where, near_mine, near_other, passed, old_mine, old_other):
    return pl.pallas_call(
        passed_kernel,
        in_specs=[smem()] + [vmem()] * 5,
        out_specs=[vmem()] * 2,
        out_shape=[jax.ShapeDtypeStruct(old_mine.shape, F32)] * 2,
        compiler_params=params(PASSED),
        name="passed",
    )(where, near_mine, near_other, passed, old_mine, old_other)


def last_forward(far, weights, before):
    return pl.pallas_call(
        last_kernel,
        in_specs=[vmem()] * 3,
        out_specs=vmem(),
        out_shape=jax.ShapeDtypeStruct(before.shape, F32),
        compiler_params=params(LAST),
        name="last",
    )(far, weights, before)


def plane_gather(w):
    return lax.all_to_all(jnp.broadcast_to(w[None], (X * Y,) + w.shape), XY, 0, 0)


def middle_kernel(mine_ref, other_ref, hidden_ref, read_ref, mask_ref, up_ref, out_ref):
    tokens, features = read_ref.shape
    rank = up_ref.shape[0] // 2
    base = mine_ref[:, :features] + other_ref[:, :features]
    low = mine_ref[:, features:] + other_ref[:, features:]
    low_b = low.astype(BF16)
    policy = base + ADAPTER_SCALE * jnp.dot(low_b, up_ref[...], preferred_element_type=F32)
    read = read_ref[...].astype(F32)
    sign = jnp.where(lax.broadcasted_iota(jnp.int32, (tokens, 1), 0) < tokens // 2, 1.0, -1.0)
    signed = mask_ref[...] * sign
    t_pol = jnp.tanh(policy)
    t_ref = jnp.tanh(base)
    scores = jnp.sum(read * (t_pol - t_ref), axis=1, keepdims=True) * signed
    total = jnp.sum(scores, axis=0, keepdims=True)
    grad = ((-DPO_BETA * signed) * read * (1.0 - t_pol * t_pol)).astype(BF16)
    low_grad_t = (
        ADAPTER_SCALE
        * lax.dot_general(up_ref[:rank, :], grad, (((1,), (1,)), ((), ())), preferred_element_type=F32)
    ).astype(BF16)
    twice = (low + pltpu.roll(low, rank, 1)).astype(BF16)
    up_grad = ADAPTER_SCALE * lax.dot_general(
        grad, twice, (((0,), (0,)), ((), ())), preferred_element_type=F32
    )
    wide = 2 * LANES
    part = features // (X * ZH * Y)
    lane = lax.broadcasted_iota(jnp.int32, (EXTRA, LANES), 1)
    sent = pieces(total, (EXTRA, LANES)).astype(BF16)
    for x in range(X):
        for y in range(Y):
            to = x * Y + y
            places = [(x * ZH + zh) * Y + y for zh in range(ZH)]
            for zh, s in enumerate(places):
                out_ref[to, zh * rank : (zh + 1) * rank, :] = jnp.dot(
                    low_grad_t, hidden_ref[:, s * wide : (s + 1) * wide], preferred_element_type=F32
                ).astype(BF16)
            both = jnp.where(
                lane < rank,
                up_grad[places[0] * part : (places[0] + 1) * part, :],
                up_grad[places[1] * part : (places[1] + 1) * part, :],
            )
            out_ref[to, ZH * rank :, :LANES] = both.astype(BF16)
            out_ref[to, ZH * rank :, LANES:] = sent


def plane_kernel(got_ref, out_ref):
    rank = (got_ref.shape[1] - EXTRA) // ZH
    rows = rank // ZL
    total = got_ref[0].astype(F32)
    for s in range(1, got_ref.shape[0]):
        total = total + got_ref[s].astype(F32)
    first = ZH * rank
    margin = jnp.sum(total[first : first + 1, LANES:], axis=1, keepdims=True)
    sent = pieces(margin, (8, LANES))
    lane = lax.broadcasted_iota(jnp.int32, (8, LANES), 1)
    upper = total[first : first + 8, :LANES]
    lower = total[first + 8 : first + 16, :LANES]
    packed = [
        jnp.where(lane < rank, upper, pltpu.roll(lower, rank, 1)),
        jnp.where(lane < rank, pltpu.roll(upper, rank, 1), lower),
    ]
    for zl in range(ZL):
        for zh in range(ZH):
            start = zh * rank + zl * rows
            tail = jnp.concatenate([packed[zh], sent], axis=1)
            out_ref[zl * ZH + zh] = jnp.concatenate(
                [total[start : start + rows, :], tail], axis=0
            ).astype(BF16)


def gate_kernel(got_ref, out_ref, diff_ref):
    total = None
    for zl in range(ZL):
        pair = got_ref[zl * ZH].astype(F32) + got_ref[zl * ZH + 1].astype(F32)
        diff = jnp.sum(pair[8:9, LANES:], axis=1, keepdims=True)
        gate = 1.0 / (1.0 + jnp.exp(DPO_BETA * diff))
        total = gate * pair if total is None else total + gate * pair
        diff_ref[zl : zl + 1, :] = jnp.broadcast_to(diff, (1, LANES))
    out_ref[...] = total


def shards(hidden_input, readout, response, value_matrix, adapter_down, adapter_up):
    seq_rows, width = hidden_input.shape[2:]
    tokens = 2 * seq_rows
    features = value_matrix.shape[1]
    rank = adapter_down.shape[1]
    core, zh, zl = lax.axis_index("core"), lax.axis_index("zh"), lax.axis_index("zl")
    hidden = hidden_input.reshape(tokens, width)

    value_half = lax.dynamic_slice_in_dim(value_matrix, core * LANES, LANES, 0)
    down_half = lax.dynamic_slice_in_dim(adapter_down, core * LANES, LANES, 0)
    packed = down_half.T.reshape(features // LANES, EXTRA, LANES).transpose(1, 0, 2).reshape(EXTRA, features)
    weights = jnp.concatenate([value_half, packed], axis=0)
    sizes = (ZL, 2, X, ZH, Y)
    axes = ("zl", "core", "x", "zh", "y")
    spots = list(np.ndindex(*sizes))
    flat = lambda p: int(np.ravel_multi_index(p, sizes))

    mirror = [(flat((a, c, b, e, d)), flat((ZL - 1 - a, c, b, 1 - e, d))) for a, c, b, e, d in spots]
    swap_core = [(0, 1), (1, 0)]
    odd = zl % 2
    half = features // 2

    weights_far = lax.ppermute(weights, axes, mirror)
    near = plane_gather(lax.dynamic_slice_in_dim(weights, odd * half, half, 1))
    where = jnp.stack([core, zh, odd]).astype(jnp.int32)
    other = lax.ppermute(hidden, "core", swap_core)

    weights_far, near = lax.optimization_barrier((weights_far, near))
    far = plane_gather(weights_far)
    passed = lax.ppermute(near, "zl", [(a, a ^ 1) for a in range(ZL)])
    before_mine, before_other, near_mine, near_other, far_mine, far_other = own_forward(where, hidden, other, near)
    before_mine, before_other = passed_forward(where, near_mine, near_other, passed, before_mine, before_other)
    part_other = last_forward(far_other, far, before_other)
    from_other = lax.ppermute(part_other, "core", swap_core)
    part_mine = last_forward(far_mine, far, before_mine)

    read = readout.reshape(tokens, features)
    mask = response.reshape(tokens, 1).astype(F32)
    up = jnp.pad(adapter_up, ((0, rank), (0, 0)))
    wide = width // (X * ZH * Y)
    sends = pl.pallas_call(
        middle_kernel,
        in_specs=[vmem()] * 6,
        out_specs=vmem(),
        out_shape=jax.ShapeDtypeStruct((X * Y, ZH * rank + EXTRA, wide), BF16),
        compiler_params=params(MIDDLE),
        name="middle",
    )(part_mine, from_other, hidden, read, mask, up)
    got = lax.all_to_all(sends, XY, 0, 0)
    along = pl.pallas_call(
        plane_kernel,
        in_specs=[vmem()],
        out_specs=vmem(),
        out_shape=jax.ShapeDtypeStruct((ZL * ZH, 16, wide), BF16),
        compiler_params=params(),
        name="plane",
    )(got)
    got = lax.all_to_all(along, ZZ, 0, 0)
    gated, diffs = pl.pallas_call(
        gate_kernel,
        in_specs=[vmem()],
        out_specs=[vmem(), vmem()],
        out_shape=[jax.ShapeDtypeStruct((16, wide), F32), jax.ShapeDtypeStruct((ZL, LANES), F32)],
        compiler_params=params(),
        name="gate",
    )(got)
    summed, diffs = lax.optimization_barrier((lax.psum(gated, "core"), diffs))
    rows = rank // ZL
    all_rows = lax.all_to_all(jnp.broadcast_to(summed[None, :rows], (ZL, rows, wide)), "zl", 0, 0)
    down_gradient = all_rows.reshape(rank, wide).T
    up_part = jnp.concatenate([summed[8:16, :rank], summed[8:16, rank : 2 * rank]], axis=0)
    margin = DPO_BETA * lax.dynamic_slice(diffs, (zl, 0), (1, 1)).reshape(1)
    return down_gradient, up_part, jax.nn.softplus(-margin), margin


def solution(mesh):
    fine = Mesh(np.asarray(mesh.devices).reshape(ZL, 2, X, ZH, Y), ("zl", "core", "x", "zh", "y"))
    dp, fsdp = ("zl", "core"), ("x", "zh", "y")
    placed = (
        P(dp, None, fsdp, None),
        P(dp, None, fsdp, None),
        P(dp, None, fsdp),
        P(fsdp, None),
        P(fsdp, None),
        P(),
    )
    return jax.shard_map(
        shards,
        mesh=fine,
        in_specs=placed,
        out_specs=(P(fsdp, None), P(fsdp, None), P(dp), P(dp)),
        check_vma=False,
    )
```

```python
import jax
import jax.numpy as jnp
import numpy as np
from jax import lax
from jax.experimental import pallas as pl
from jax.experimental.pallas import tpu as pltpu
from jax.sharding import Mesh, PartitionSpec as P

DPO_BETA = 0.5
ADAPTER_SCALE = 2.0
BF16 = jnp.bfloat16
F32 = jnp.float32
LANES = 128
X, Y, ZH, ZL = 4, 4, 2, 8
XY = ("x", "y")
ZZ = ("zl", "zh")
EXTRA = 16
OWN, PASSED, LAST, MIDDLE = 50, 20, 20, 20


def vmem():
    return pl.BlockSpec(memory_space=pltpu.VMEM)


def params(mib=50):
    return pltpu.CompilerParams(vmem_limit_bytes=mib * 1024 * 1024)


def pieces(total, shape):
    full = jnp.broadcast_to(total, shape)
    high = full.astype(BF16).astype(F32)
    rest = full - high
    middle = rest.astype(BF16).astype(F32)
    low = rest - middle
    lane = lax.broadcasted_iota(jnp.int32, shape, 1)
    zero = jnp.zeros(shape, F32)
    return jnp.where(lane == 0, high, jnp.where(lane == 1, middle, jnp.where(lane == 2, low, zero)))


def anywhere():
    return pl.BlockSpec(memory_space=pl.ANY)


def fetches(where_ref, hidden_ref, buffer, sems, far):
    core = where_ref[0]
    zh = 1 - where_ref[1] if far else where_ref[1]
    copies = []
    for x in range(X):
        for y in range(Y):
            at = x * Y + y
            start = (((x * ZH + zh) * Y + y) * 2 + core) * LANES
            copies.append(
                pltpu.make_async_copy(
                    hidden_ref.at[:, pl.ds(pl.multiple_of(start, LANES), LANES)],
                    buffer.at[:, at * LANES : (at + 1) * LANES],
                    sems.at[at],
                )
            )
    return copies


def unpacked(weight_ref):
    sources, _, features = weight_ref.shape
    value = weight_ref[:, :LANES, :].reshape(sources * LANES, features)
    down_t = [
        jnp.concatenate([weight_ref[s, LANES:, g * LANES : (g + 1) * LANES] for s in range(sources)], axis=1)
        for g in range(features // LANES)
    ]
    return value, jnp.concatenate(down_t, axis=0)


def low_part(hidden, down_t):
    down_t = jnp.concatenate([down_t, jnp.zeros((LANES - down_t.shape[0], down_t.shape[1]), BF16)], axis=0)
    return lax.dot_general(hidden, down_t, (((1,), (1,)), ((), ())), preferred_element_type=F32)


def own_kernel(where_ref, mine_ref, other_ref, own_ref, *refs):
    out_mine_ref, out_other_ref, near_mine, near_other, far_mine, far_other, sems = refs
    held = ((mine_ref, near_mine, False), (other_ref, near_other, False), (mine_ref, far_mine, True), (other_ref, far_other, True))
    copies = [
        copy
        for at, (ref, block_ref, far) in enumerate(held)
        for copy in fetches(where_ref, ref, block_ref, sems.at[at], far)
    ]
    for copy in copies:
        copy.start()
    for copy in copies:
        copy.wait()
    half = own_ref.shape[2]
    value, down_t = unpacked(own_ref)
    nothing = jnp.zeros_like(down_t)

    def body(columns, rest, down_t):
        for ref, out_ref in ((near_mine, out_mine_ref), (near_other, out_other_ref)):
            hidden = ref[...]
            out_ref[:, columns] = jnp.dot(hidden, value, preferred_element_type=F32)
            out_ref[:, rest] = jnp.zeros((hidden.shape[0], half), F32)
            out_ref[:, 2 * half :] = low_part(hidden, down_t)

    @pl.when(where_ref[2] == 0)
    def _():
        body(slice(0, half), slice(half, 2 * half), jnp.concatenate([down_t, nothing], axis=0))

    @pl.when(where_ref[2] != 0)
    def _():
        body(slice(half, 2 * half), slice(0, half), jnp.concatenate([nothing, down_t], axis=0))


def passed_kernel(where_ref, mine_ref, other_ref, passed_ref, old_mine_ref, old_other_ref, new_mine_ref, new_other_ref):
    half = passed_ref.shape[2]
    value, down_t = unpacked(passed_ref)
    nothing = jnp.zeros_like(down_t)

    def body(columns, rest, down_t):
        for near_ref, old_ref, new_ref in (
            (mine_ref, old_mine_ref, new_mine_ref),
            (other_ref, old_other_ref, new_other_ref),
        ):
            near = near_ref[...]
            new_ref[:, columns] = old_ref[:, columns] + jnp.dot(near, value, preferred_element_type=F32)
            new_ref[:, rest] = old_ref[:, rest]
            new_ref[:, 2 * half :] = old_ref[:, 2 * half :] + low_part(near, down_t)

    @pl.when(where_ref[2] == 0)
    def _():
        body(slice(half, 2 * half), slice(0, half), jnp.concatenate([nothing, down_t], axis=0))

    @pl.when(where_ref[2] != 0)
    def _():
        body(slice(0, half), slice(half, 2 * half), jnp.concatenate([down_t, nothing], axis=0))


def last_kernel(far_ref, weight_ref, before_ref, out_ref):
    features = weight_ref.shape[2]
    value, down_t = unpacked(weight_ref)
    far = far_ref[...]
    out_ref[:, :features] = before_ref[:, :features] + jnp.dot(far, value, preferred_element_type=F32)
    out_ref[:, features:] = before_ref[:, features:] + low_part(far, down_t)


def smem():
    return pl.BlockSpec(memory_space=pltpu.SMEM)


def own_forward(where, mine, other, own):
    tokens, width = mine.shape
    out = jax.ShapeDtypeStruct((tokens, 2 * own.shape[2] + LANES), F32)
    block = jax.ShapeDtypeStruct((tokens, width // 4), BF16)
    return pl.pallas_call(
        own_kernel,
        in_specs=[smem(), anywhere(), anywhere(), vmem()],
        out_specs=[vmem()] * 6,
        out_shape=[out] * 2 + [block] * 4,
        scratch_shapes=[pltpu.SemaphoreType.DMA((4, X * Y))],
        compiler_params=params(OWN),
        name="own",
    )(where, mine, other, own)


def passed_forward(where, near_mine, near_other, passed, old_mine, old_other):
    return pl.pallas_call(
        passed_kernel,
        in_specs=[smem()] + [vmem()] * 5,
        out_specs=[vmem()] * 2,
        out_shape=[jax.ShapeDtypeStruct(old_mine.shape, F32)] * 2,
        compiler_params=params(PASSED),
        name="passed",
    )(where, near_mine, near_other, passed, old_mine, old_other)


def last_forward(far, weights, before):
    return pl.pallas_call(
        last_kernel,
        in_specs=[vmem()] * 3,
        out_specs=vmem(),
        out_shape=jax.ShapeDtypeStruct(before.shape, F32),
        compiler_params=params(LAST),
        name="last",
    )(far, weights, before)


def plane_gather(w):
    return lax.all_to_all(jnp.broadcast_to(w[None], (X * Y,) + w.shape), XY, 0, 0)


def middle_kernel(mine_ref, other_ref, hidden_ref, read_ref, mask_ref, up_ref, out_ref):
    tokens, features = read_ref.shape
    rank = up_ref.shape[0] // 2
    base = mine_ref[:, :features] + other_ref[:, :features]
    low = mine_ref[:, features:] + other_ref[:, features:]
    low_b = low.astype(BF16)
    policy = base + ADAPTER_SCALE * jnp.dot(low_b, up_ref[...], preferred_element_type=F32)
    read = read_ref[...].astype(F32)
    sign = jnp.where(lax.broadcasted_iota(jnp.int32, (tokens, 1), 0) < tokens // 2, 1.0, -1.0)
    signed = mask_ref[...] * sign
    t_pol = jnp.tanh(policy)
    t_ref = jnp.tanh(base)
    scores = jnp.sum(read * (t_pol - t_ref), axis=1, keepdims=True) * signed
    total = jnp.sum(scores, axis=0, keepdims=True)
    grad = ((-DPO_BETA * signed) * read * (1.0 - t_pol * t_pol)).astype(BF16)
    low_grad_t = (
        ADAPTER_SCALE
        * lax.dot_general(up_ref[:rank, :], grad, (((1,), (1,)), ((), ())), preferred_element_type=F32)
    ).astype(BF16)
    twice = (low + pltpu.roll(low, rank, 1)).astype(BF16)
    up_grad = ADAPTER_SCALE * lax.dot_general(
        grad, twice, (((0,), (0,)), ((), ())), preferred_element_type=F32
    )
    wide = 2 * LANES
    part = features // (X * ZH * Y)
    lane = lax.broadcasted_iota(jnp.int32, (EXTRA, LANES), 1)
    sent = pieces(total, (EXTRA, LANES)).astype(BF16)
    for x in range(X):
        for y in range(Y):
            to = x * Y + y
            places = [(x * ZH + zh) * Y + y for zh in range(ZH)]
            for zh, s in enumerate(places):
                out_ref[to, zh * rank : (zh + 1) * rank, :] = jnp.dot(
                    low_grad_t, hidden_ref[:, s * wide : (s + 1) * wide], preferred_element_type=F32
                ).astype(BF16)
            both = jnp.where(
                lane < rank,
                up_grad[places[0] * part : (places[0] + 1) * part, :],
                up_grad[places[1] * part : (places[1] + 1) * part, :],
            )
            out_ref[to, ZH * rank :, :LANES] = both.astype(BF16)
            out_ref[to, ZH * rank :, LANES:] = sent


def plane_kernel(got_ref, out_ref):
    rank = (got_ref.shape[1] - EXTRA) // ZH
    rows = rank // ZL
    total = got_ref[0].astype(F32)
    for s in range(1, got_ref.shape[0]):
        total = total + got_ref[s].astype(F32)
    first = ZH * rank
    margin = jnp.sum(total[first : first + 1, LANES:], axis=1, keepdims=True)
    sent = pieces(margin, (8, LANES))
    lane = lax.broadcasted_iota(jnp.int32, (8, LANES), 1)
    upper = total[first : first + 8, :LANES]
    lower = total[first + 8 : first + 16, :LANES]
    packed = [
        jnp.where(lane < rank, upper, pltpu.roll(lower, rank, 1)),
        jnp.where(lane < rank, pltpu.roll(upper, rank, 1), lower),
    ]
    for zl in range(ZL):
        for zh in range(ZH):
            start = zh * rank + zl * rows
            tail = jnp.concatenate([packed[zh], sent], axis=1)
            out_ref[zl * ZH + zh] = jnp.concatenate(
                [total[start : start + rows, :], tail], axis=0
            ).astype(BF16)


def gate_kernel(got_ref, out_ref, diff_ref):
    total = None
    for zl in range(ZL):
        pair = got_ref[zl * ZH].astype(F32) + got_ref[zl * ZH + 1].astype(F32)
        diff = jnp.sum(pair[8:9, LANES:], axis=1, keepdims=True)
        gate = 1.0 / (1.0 + jnp.exp(DPO_BETA * diff))
        total = gate * pair if total is None else total + gate * pair
        diff_ref[zl : zl + 1, :] = jnp.broadcast_to(diff, (1, LANES))
    out_ref[...] = total


def shards(hidden_input, readout, response, value_matrix, adapter_down, adapter_up):
    seq_rows, width = hidden_input.shape[2:]
    tokens = 2 * seq_rows
    features = value_matrix.shape[1]
    rank = adapter_down.shape[1]
    core, zh, zl = lax.axis_index("core"), lax.axis_index("zh"), lax.axis_index("zl")
    hidden = hidden_input.reshape(tokens, width)

    value_half = lax.dynamic_slice_in_dim(value_matrix, core * LANES, LANES, 0)
    down_half = lax.dynamic_slice_in_dim(adapter_down, core * LANES, LANES, 0)
    packed = down_half.T.reshape(features // LANES, EXTRA, LANES).transpose(1, 0, 2).reshape(EXTRA, features)
    weights = jnp.concatenate([value_half, packed], axis=0)
    sizes = (ZL, 2, X, ZH, Y)
    axes = ("zl", "core", "x", "zh", "y")
    spots = list(np.ndindex(*sizes))
    flat = lambda p: int(np.ravel_multi_index(p, sizes))

    mirror = [(flat((a, c, b, e, d)), flat((ZL - 1 - a, c, b, 1 - e, d))) for a, c, b, e, d in spots]
    swap_core = [(0, 1), (1, 0)]
    odd = zl % 2
    half = features // 2

    weights_far = lax.ppermute(weights, axes, mirror)
    near = plane_gather(lax.dynamic_slice_in_dim(weights, odd * half, half, 1))
    where = jnp.stack([core, zh, odd]).astype(jnp.int32)
    other = lax.ppermute(hidden, "core", swap_core)

    weights_far, near = lax.optimization_barrier((weights_far, near))
    far = plane_gather(weights_far)
    passed = lax.ppermute(near, "zl", [(a, a ^ 1) for a in range(ZL)])
    before_mine, before_other, near_mine, near_other, far_mine, far_other = own_forward(where, hidden, other, near)
    before_mine, before_other = passed_forward(where, near_mine, near_other, passed, before_mine, before_other)
    part_other = last_forward(far_other, far, before_other)
    from_other = lax.ppermute(part_other, "core", swap_core)
    part_mine = last_forward(far_mine, far, before_mine)

    read = readout.reshape(tokens, features)
    mask = response.reshape(tokens, 1).astype(F32)
    up = jnp.pad(adapter_up, ((0, rank), (0, 0)))
    wide = width // (X * ZH * Y)
    sends = pl.pallas_call(
        middle_kernel,
        in_specs=[vmem()] * 6,
        out_specs=vmem(),
        out_shape=jax.ShapeDtypeStruct((X * Y, ZH * rank + EXTRA, wide), BF16),
        compiler_params=params(MIDDLE),
        name="middle",
    )(part_mine, from_other, hidden, read, mask, up)
    got = lax.all_to_all(sends, XY, 0, 0)
    along = pl.pallas_call(
        plane_kernel,
        in_specs=[vmem()],
        out_specs=vmem(),
        out_shape=jax.ShapeDtypeStruct((ZL * ZH, 16, wide), BF16),
        compiler_params=params(),
        name="plane",
    )(got)
    got = lax.all_to_all(along, ZZ, 0, 0)
    gated, diffs = pl.pallas_call(
        gate_kernel,
        in_specs=[vmem()],
        out_specs=[vmem(), vmem()],
        out_shape=[jax.ShapeDtypeStruct((16, wide), F32), jax.ShapeDtypeStruct((ZL, LANES), F32)],
        compiler_params=params(),
        name="gate",
    )(got)
    rows = rank // ZL
    copies = jnp.broadcast_to(gated[None, :rows], (ZL * 2, rows, wide))
    all_rows = lax.all_to_all(copies, ("zl", "core"), 0, 0)
    down_gradient = jnp.sum(all_rows.reshape(ZL, 2, rows, wide), axis=1).reshape(rank, wide).T
    summed = lax.psum(gated[8:, : 2 * rank], "core")
    up_part = jnp.concatenate([summed[:, :rank], summed[:, rank:]], axis=0)
    margin = DPO_BETA * lax.dynamic_slice(diffs, (zl, 0), (1, 1)).reshape(1)
    return down_gradient, up_part, jax.nn.softplus(-margin), margin


def solution(mesh):
    fine = Mesh(np.asarray(mesh.devices).reshape(ZL, 2, X, ZH, Y), ("zl", "core", "x", "zh", "y"))
    dp, fsdp = ("zl", "core"), ("x", "zh", "y")
    placed = (
        P(dp, None, fsdp, None),
        P(dp, None, fsdp, None),
        P(dp, None, fsdp),
        P(fsdp, None),
        P(fsdp, None),
        P(),
    )
    return jax.shard_map(
        shards,
        mesh=fine,
        in_specs=placed,
        out_specs=(P(fsdp, None), P(fsdp, None), P(dp), P(dp)),
        check_vma=False,
    )
```
